32 devices in a mesh: ctx: 32 (over z, y, x, core), tp: 1.
Axes of the slice: x: 2, y: 2, z: 4, core: 2. Of those that a mesh axis runs over, the one named last changes fastest.
Arguments:
- query_in: bfloat16 [8192, 2048], P('ctx', 'tp'), may hold values from -6 to 6
- key_in: bfloat16 [8192, 2048], P('ctx', 'tp'), may hold values from -6 to 6
- value_in: bfloat16 [8192, 4096], P('ctx', 'tp'), may hold values from -6 to 6
- gate_values: bfloat16 [8192, 4096], P('ctx', 'tp'), may hold values from -6 to 6
- query_conv: bfloat16 [4, 2048], P(None, 'tp'), may hold values from -3 to 3
- key_conv: bfloat16 [4, 2048], P(None, 'tp'), may hold values from -3 to 3
- value_conv: bfloat16 [4, 4096], P(None, 'tp'), may hold values from -3 to 3
- beta_rate: float32 [32, 8192], P('tp', 'ctx'), may hold values from 0.002 to 0.9, as said below
- log_decay: float32 [32, 8192], P('tp', 'ctx'), may hold values from -0.8 to 0, as said below
- norm_gain: float32 [128], replicated, may hold values from 0.1 to 1.9
- out_weight: bfloat16 [4096, 2048], P('tp'), may hold values from -0.09375 to 0.09375
Outputs:
- layer_out: bfloat16 [8192, 2048], P(('ctx', 'tp'))
The draws below stay inside these ranges and needn't reach their ends.
Inputs may be any that keep to these rules, and one draw needn't show every extreme that they name: beta_rate lies strictly between 0 and 1. log_decay is never positive.
All inputs are finite; a program needn't handle non-finite values.
Results may differ from the reference program's by a relative error of at most 0.014.
Values may be sent and summed in bfloat16 or wider, within the bound.
A program may use at most 256 MiB of HBM per device.

```python
import jax
import jax.numpy as jnp
from jax import lax

D = 2048
HK = 16
HV = 32
DK = 128
DV = 128
KW = 4
BLOCK = 64
TOKENS = 8192
N_TP = 1


def head_kinds(key, cutoff):
    labels = jax.random.randint(jax.random.fold_in(key, 11), (HV,), 0, 8)
    return labels < cutoff


def draw_beta_rate(key, part):
    cutoff = 4
    is_fast = head_kinds(key, cutoff)
    uniform_draw = jax.random.uniform(jax.random.fold_in(key, 21), (HV, TOKENS), jnp.float32)
    fast_rate = 0.3 + 0.6 * uniform_draw
    slow_rate = 0.002 * jnp.exp(uniform_draw * jnp.log(10.0))
    return jnp.where(is_fast[:, None], fast_rate, slow_rate).astype(jnp.float32)


def draw_log_decay(key, part):
    cutoff = 4
    is_fast = head_kinds(key, cutoff)
    jitter = jnp.exp(jax.random.uniform(jax.random.fold_in(key, 41), (HV, TOKENS), jnp.float32, -0.69, 0.69))
    block_scale = jnp.exp(jax.random.uniform(jax.random.fold_in(key, 42), (HV, 16), jnp.float32, -0.69, 0.69))
    block_scale = jnp.repeat(block_scale, TOKENS // 16, axis=1)
    base_rate = jnp.where(is_fast[:, None], 1.0 / 40.0, 0.5 / TOKENS)
    beta_strength = base_rate * jitter * block_scale
    token_positions = jax.random.randint(jax.random.fold_in(key, 43), (HV, 4, 1), 0, TOKENS)
    token_places = lax.broadcasted_iota(jnp.int32, (HV, 4, TOKENS), 2)
    token_groups_list = jnp.any(token_places == token_positions, axis=1)
    layer_depth = jax.random.uniform(jax.random.fold_in(key, 44), (HV, TOKENS), jnp.float32, 0.22, 0.69)
    return (-(beta_strength + jnp.where(token_groups_list, layer_depth, 0.0))).astype(jnp.float32)


def steps_of(stream_key, dims, pieces, least, high):
    factor_of, own = 1.0, jax.random.fold_in(stream_key, 6)
    for dim, shards_of in pieces:
        heights = jnp.exp(jax.random.uniform(jax.random.fold_in(own, dim), (shards_of,), jnp.float32, least / len(pieces), high / len(pieces)))
        factor_of = factor_of * jnp.repeat(heights, dims[dim] // shards_of).reshape([-1 if axis == dim else 1 for axis in range(len(dims))])
    return factor_of


def bell_draw(own_key, extent, scale, most, pieces=(), kind=jnp.bfloat16):
    drawn = jax.random.normal(own_key, extent, jnp.float32) * scale
    if len(pieces) > 0:
        drawn = steps_of(own_key, extent, pieces, -0.22, 0.18) * drawn
    return jnp.clip(drawn, min=-most, max=most).astype(kind)


def setup_inputs(seed: int = 0) -> dict:
    key_list = jax.random.split(jax.random.key(seed), 12)
    return {
        "query_in": bell_draw(key_list[0], (TOKENS, HK * DK), 1.0, 6.0, ((0, 32),)),
        "key_in": bell_draw(key_list[1], (TOKENS, HK * DK), 1.0, 6.0, ((0, 32),)),
        "value_in": bell_draw(key_list[2], (TOKENS, HV * DV), 1.0, 6.0, ((0, 32),)),
        "gate_values": bell_draw(key_list[3], (TOKENS, HV * DV), 1.0, 6.0, ((0, 32),)),
        "query_conv": bell_draw(key_list[4], (KW, HK * DK), KW ** -0.5, 3.0),
        "key_conv": bell_draw(key_list[5], (KW, HK * DK), KW ** -0.5, 3.0),
        "value_conv": bell_draw(key_list[6], (KW, HV * DV), KW ** -0.5, 3.0),
        "beta_rate": draw_beta_rate(jax.random.fold_in(key_list[11], 71), 0),
        "log_decay": draw_log_decay(jax.random.fold_in(key_list[11], 71), 0),
        "norm_gain": jnp.clip(1.0 + 0.18 * jax.random.normal(key_list[9], (DV,), jnp.float32), 0.1, 1.9),
        "out_weight": bell_draw(key_list[10], (HV * DV, D), (HV * DV) ** -0.5, 0.09375),
    }


precise = lax.Precision.HIGHEST

def pairwise_dot_entries(form, left, right):
    return jnp.einsum(form, left, right, precision=precise)

def causal_conv(rim_rows, raw_rows, tap_weights):
    joined = jnp.concatenate([rim_rows, raw_rows], axis=0).astype(jnp.float32)
    taps = tap_weights.astype(jnp.float32)
    row_count = raw_rows.shape[0]
    running = taps[0] * joined[0:row_count]
    for offset in range(1, tap_weights.shape[0]):
        running = running + taps[offset] * joined[offset:offset + row_count]
    return jax.nn.silu(running)

def unit_rows(key_rows):
    return key_rows * lax.rsqrt(lax.optimization_barrier(jnp.sum(key_rows * key_rows, axis=-1, keepdims=True)) + 1e-06)

def block_prep(probe_vectors, key_rows, values, strength, decay):
    block_size = decay.shape[-1]
    cumulative = jnp.cumsum(decay, axis=-1)
    row_index = lax.broadcasted_iota(jnp.int32, (block_size, block_size), 0)
    col_index = lax.broadcasted_iota(jnp.int32, (block_size, block_size), 1)
    spread = cumulative[..., :, None] - cumulative[..., None, :]
    fading = jnp.where(row_index >= col_index, jnp.exp(jnp.minimum(spread, 0.0)), 0.0)
    inner_dots = pairwise_dot_entries('...ik,...jk->...ij', key_rows, key_rows)
    lower_part = jnp.where(row_index > col_index, strength[..., :, None] * fading * inner_dots, 0.0)
    unit_lower = jnp.eye(block_size, dtype=jnp.float32) + lower_part
    cumulative_forget_ratio = jnp.exp(cumulative)
    stacked = jnp.concatenate([strength[..., None] * values, (strength * cumulative_forget_ratio)[..., None] * key_rows], axis=-1)
    solved = jax.scipy.linalg.solve_triangular(unit_lower, stacked, lower=True, unit_diagonal=True)
    value_width = values.shape[-1]
    state_updates = solved[..., :value_width]
    weight_params = solved[..., value_width:]
    causal_similarity_matrix = jnp.where(row_index >= col_index, fading * pairwise_dot_entries('...ik,...jk->...ij', probe_vectors, key_rows), 0.0)
    block_decay_factor = cumulative_forget_ratio[..., -1]
    decayed_tail_keys = jnp.exp(cumulative[..., -1:] - cumulative)[..., None] * key_rows
    return (probe_vectors, state_updates, weight_params, causal_similarity_matrix, cumulative_forget_ratio, decayed_tail_keys, block_decay_factor)

def block_step(running_recurrent_summary, block_data):
    probe_vectors, state_updates, weight_params, causal_similarity_matrix, cumulative_forget_ratio, decayed_tail_keys, block_decay_factor = block_data
    residual_target_vectors = state_updates - pairwise_dot_entries('ret,rtw->rew', weight_params, running_recurrent_summary)
    emitted_vectors = cumulative_forget_ratio[..., None] * pairwise_dot_entries('ret,rtw->rew', probe_vectors, running_recurrent_summary) + pairwise_dot_entries('keo,kov->kev', causal_similarity_matrix, residual_target_vectors)
    running_recurrent_summary = block_decay_factor[:, None, None] * running_recurrent_summary + pairwise_dot_entries('dwn,dwm->dnm', decayed_tail_keys, residual_target_vectors)
    return (running_recurrent_summary, emitted_vectors)

def gate_norm(core_out, gate_values, norm_gain):
    gate_part = gate_values.astype(jnp.float32).reshape(core_out.shape)
    scaling = lax.rsqrt(lax.optimization_barrier(jnp.mean(core_out * core_out, axis=-1, keepdims=True)) + 1e-06)
    gated = (core_out * scaling * norm_gain * jax.nn.silu(gate_part)).astype(jnp.bfloat16)
    return gated.reshape(core_out.shape[0], core_out.shape[1] * core_out.shape[2])

def reference(query_in, key_in, value_in, gate_values, query_conv, key_conv, value_conv, beta_rate, log_decay, norm_gain, out_weight):
    head_ratio = HV // HK
    block_count = TOKENS // BLOCK

    def convolve(raw_rows, tap_weights):
        rim_rows = jnp.zeros((tap_weights.shape[0] - 1, raw_rows.shape[1]), raw_rows.dtype)
        return causal_conv(rim_rows, raw_rows, tap_weights)
    probe_vectors = convolve(query_in, query_conv).reshape(block_count, BLOCK, HK, DK).transpose(0, 2, 1, 3)
    key_rows = unit_rows(convolve(key_in, key_conv).reshape(block_count, BLOCK, HK, DK)).transpose(0, 2, 1, 3)
    values = convolve(value_in, value_conv).reshape(block_count, BLOCK, HV, DV).transpose(0, 2, 1, 3)
    strength = beta_rate.reshape(HV, block_count, BLOCK).transpose(1, 0, 2)
    decay = log_decay.reshape(HV, block_count, BLOCK).transpose(1, 0, 2)

    def advance(running_recurrent_summary, block_data):
        query_block, key_block, value_block, strength_block, decay_block = block_data
        prepared = block_prep(jnp.repeat(query_block, head_ratio, axis=0), jnp.repeat(key_block, head_ratio, axis=0), value_block, strength_block, decay_block)
        return block_step(running_recurrent_summary, prepared)
    zero_state = jnp.zeros((HV, DK, DV), jnp.float32)
    final_state, emitted_vectors = lax.scan(advance, zero_state, (probe_vectors, key_rows, values, strength, decay))
    core_out = emitted_vectors.transpose(0, 2, 1, 3).reshape(TOKENS, HV, DV)
    gated = gate_norm(core_out, gate_values, norm_gain)
    group_cols = HV * DV // N_TP
    running = jnp.zeros((TOKENS, D), jnp.float32)
    for member in range(N_TP):
        partial_sum = jnp.dot(gated[:, member * group_cols:(member + 1) * group_cols].astype(jnp.float32), out_weight[member * group_cols:(member + 1) * group_cols].astype(jnp.float32), preferred_element_type=jnp.float32)
        rounded = lax.optimization_barrier(partial_sum.astype(jnp.bfloat16))
        running = running + rounded.astype(jnp.float32)
    return running.astype(jnp.bfloat16)
```

```python
import functools
import math

import jax
import jax.numpy as jnp
from jax import lax
from jax.experimental import pallas as pl
from jax.experimental.pallas import tpu as pltpu
from jax.sharding import PartitionSpec as P

HK = 16
HV = 32
DK = 128
DV = 128
SUB = 128
PAD = 8
EXTRA = 16
MESH = pl.DeviceIdType.MESH
f32 = jnp.float32
bf16 = jnp.bfloat16


def mm(a, b):
    return jnp.dot(a.astype(bf16), b.astype(bf16), preferred_element_type=f32)


def mm_t(a, b):
    return lax.dot_general(
        a.astype(bf16), b.astype(bf16), (((1,), (1,)), ((), ())), preferred_element_type=f32
    )


def split(a):
    high = a.astype(bf16)
    return high, (a - high.astype(f32)).astype(bf16)


def silu(x):
    return x / (1.0 + jnp.exp(-x))


def conv(raw_ref, rim_ref, taps_ref, lo, hi):
    rows = raw_ref.shape[0]
    joined = jnp.concatenate([rim_ref[:, lo:hi], raw_ref[:, lo:hi].astype(f32)], axis=0)
    count = taps_ref.shape[0]
    first = PAD - count + 1
    total = taps_ref[0:1, lo:hi] * joined[first : first + rows]
    for j in range(1, count):
        total = total + taps_ref[j : j + 1, lo:hi] * joined[first + j : first + j + rows]
    return silu(total)


def unit_lower_inverses(lowers):
    size = lowers[0].shape[0]
    row = lax.broadcasted_iota(jnp.int32, (size, size), 0)
    col = lax.broadcasted_iota(jnp.int32, (size, size), 1)
    eye = (row == col).astype(f32)
    pair = ((row // 2) == (col // 2)) & (row != col)
    found = [eye - jnp.where(pair, low, 0.0) for low in lowers]
    step = 2
    while step < size:
        take = ((row // (2 * step)) == (col // (2 * step))) & ((row // step) != (col // step))
        halves = [x.astype(bf16) for x in found]
        first = [mm(jnp.where(take, low, 0.0), x) for low, x in zip(lowers, halves)]
        found = [f - mm(x, y) for f, x, y in zip(found, halves, first)]
        step *= 2
    return [x.astype(bf16) for x in found]


def maps_kernel(
    key_heads, ratio, q_ref, k_ref, v_ref, qrim, krim, vrim, qtap, ktap, vtap, col_ref, row_ref,
    emit_ref, probe_ref, msg_ref,
):
    rows = q_ref.shape[0]
    sub = min(SUB, rows)
    count = rows // sub
    row = lax.broadcasted_iota(jnp.int32, (rows, rows), 0)
    col = lax.broadcasted_iota(jnp.int32, (rows, rows), 1)
    heads = key_heads * ratio
    lowers, sims, rights, probes, tails, totals = [], [], [], [], [], []
    for g in range(key_heads):
        lo, hi = g * DK, (g + 1) * DK
        q = conv(q_ref, qrim, qtap, lo, hi)
        k = conv(k_ref, krim, ktap, lo, hi)
        k = k * lax.rsqrt(jnp.sum(k * k, axis=-1, keepdims=True) + 1e-06)
        kk = mm_t(k, k)
        qk = mm_t(q, k)
        k_turned = k.T
        for r in range(ratio):
            h = g * ratio + r
            v = conv(v_ref, vrim, vtap, h * DV, (h + 1) * DV)
            cum = col_ref[0, :, h : h + 1]
            beta = col_ref[0, :, heads + h : heads + h + 1]
            cum_row = row_ref[0, h : h + 1, :]
            fade = jnp.exp(jnp.minimum(cum - cum_row, 0.0))
            lowers.append(jnp.where(row > col, beta * fade * kk, 0.0))
            sims.append(jnp.where(row >= col, fade * qk, 0.0).astype(bf16))
            grown = jnp.exp(cum)
            rights.append(jnp.concatenate([beta * v, (beta * grown) * k], axis=1))
            probes.append(grown * q)
            last = cum_row[:, rows - 1 : rows]
            tails.append((k_turned * jnp.exp(last - cum_row)).astype(bf16))
            totals.append(jnp.exp(last))
    pieces = [
        low[i * sub : (i + 1) * sub, i * sub : (i + 1) * sub] for low in lowers for i in range(count)
    ]
    inverses = unit_lower_inverses(pieces)
    for h in range(heads):
        low = lowers[h]
        solved = []
        for i in range(count):
            right = rights[h][i * sub : (i + 1) * sub]
            if i > 0:
                before = jnp.concatenate(solved, axis=0)
                right = right - mm(low[i * sub : (i + 1) * sub, : i * sub], before)
            inverse = inverses[h * count + i]
            high, rest = split(pieces[h * count + i])
            guess = mm(inverse, right)
            guess_high, guess_rest = split(guess)
            residual = right - guess - (mm(high, guess_high) + (mm(rest, guess_high) + mm(high, guess_rest)))
            solved.append(guess + mm(inverse, residual))
        solved = jnp.concatenate(solved, axis=0).astype(bf16)
        seen = mm(sims[h], solved)
        emit_ref[:, h * DV : (h + 1) * DV] = seen[:, :DV]
        probe_ref[:, h * DK : (h + 1) * DK] = (probes[h] - seen[:, DV:]).astype(bf16)
        update = mm(tails[h], solved)
        msg_ref[h, 0:DK, :] = update[:, DV:].astype(bf16)
        msg_ref[h, DK : 2 * DK, :] = update[:, :DV].astype(bf16)
        total = jnp.broadcast_to(totals[h], (EXTRA, DV))
        high, rest = split(total)
        upper = lax.broadcasted_iota(jnp.int32, (EXTRA, DV), 0) < EXTRA // 2
        msg_ref[h, 2 * DK :, :] = jnp.where(upper, high.astype(f32), rest.astype(f32)).astype(bf16)


def local_maps(query, key, value, rims, taps, cum, beta):
    rows = query.shape[0]
    key_heads = query.shape[1] // DK
    value_heads = value.shape[1] // DV
    ratio = value_heads // key_heads
    step = math.gcd(key_heads, 2)
    groups = key_heads // step
    heads = step * ratio
    cum_rows = cum.reshape(groups, heads, rows)
    beta_rows = beta.reshape(groups, heads, rows)
    cols = jnp.concatenate([cum_rows, beta_rows], axis=1).transpose(0, 2, 1)
    wide = lambda n, width: pl.BlockSpec((n, width), lambda g: (0, g))
    kw, vw = step * DK, heads * DV
    return pl.pallas_call(
        functools.partial(maps_kernel, step, ratio),
        grid=(groups,),
        in_specs=[
            wide(rows, kw), wide(rows, kw), wide(rows, vw),
            wide(PAD, kw), wide(PAD, kw), wide(PAD, vw),
            wide(taps[0].shape[0], kw), wide(taps[1].shape[0], kw), wide(taps[2].shape[0], vw),
            pl.BlockSpec((1, rows, 2 * heads), lambda g: (g, 0, 0)),
            pl.BlockSpec((1, heads, rows), lambda g: (g, 0, 0)),
        ],
        out_specs=[
            wide(rows, vw),
            wide(rows, heads * DK),
            pl.BlockSpec((heads, 2 * DK + EXTRA, DV), lambda g: (g, 0, 0)),
        ],
        out_shape=[
            jax.ShapeDtypeStruct((rows, value_heads * DV), f32),
            jax.ShapeDtypeStruct((rows, value_heads * DK), bf16),
            jax.ShapeDtypeStruct((value_heads, 2 * DK + EXTRA, DV), bf16),
        ],
        compiler_params=pltpu.CompilerParams(vmem_limit_bytes=56 << 20),
        name="local_maps",
    )(query, key, value, *rims, *taps, cols, cum_rows)


def carry_kernel(
    n1, n2, hb, msg_ref, out_ref, got, pre_m, pre_s, pre_a, start, ready, back,
    send_sem, recv_sem, chain_send, chain_recv, back_send, back_recv,
):
    me = lax.axis_index("ctx")
    tp = lax.axis_index("tp")
    plane = me // n1
    place = me % n1
    base = plane * n1
    first, last = plane == 0, plane == n2 - 1

    def at(index):
        return (index, tp)

    barrier = pltpu.get_barrier_semaphore()
    for d in range(1, n1):
        pl.semaphore_signal(
            barrier, inc=1, device_id=at(base + (place + d) % n1), device_id_type=MESH
        )

    @pl.when(jnp.logical_not(first))
    def _():
        pl.semaphore_signal(barrier, inc=1, device_id=at(me - n1), device_id_type=MESH)

    @pl.when(jnp.logical_not(last))
    def _():
        pl.semaphore_signal(barrier, inc=1, device_id=at(me + n1), device_id_type=MESH)

    partners = n1 - 1 + jnp.where(first, 0, 1) + jnp.where(last, 0, 1)
    pl.semaphore_wait(barrier, partners)

    outgoing = []
    for d in range(1, n1):
        peer = (place + d) % n1
        copy = pltpu.make_async_remote_copy(
            src_ref=msg_ref.at[pl.ds(peer * hb, hb)],
            dst_ref=got.at[place],
            send_sem=send_sem.at[d],
            recv_sem=recv_sem.at[place],
            device_id=at(base + peer),
            device_id_type=MESH,
        )
        copy.start()
        outgoing.append(copy)
    own = pltpu.make_async_copy(msg_ref.at[pl.ds(place * hb, hb)], got.at[place], recv_sem.at[place])
    own.start()

    maps = [jnp.zeros((DK, DK), f32) for _ in range(hb)]
    states = [jnp.zeros((DK, DV), f32) for _ in range(hb)]
    fades = [jnp.ones((1, DV), f32) for _ in range(hb)]
    row = lax.broadcasted_iota(jnp.int32, (DK, DK), 0)
    col = lax.broadcasted_iota(jnp.int32, (DK, DK), 1)
    eye = (row == col).astype(f32)
    for i in range(n1):
        pltpu.make_async_copy(got.at[i], got.at[i], recv_sem.at[i]).wait()
        for h in range(hb):
            pre_m[i, h] = maps[h].astype(bf16)
            pre_s[i, h] = states[h]
            pre_a[i, h] = jnp.broadcast_to(fades[h], (8, DV))
            m = got[i, h, 0:DK, :]
            s = got[i, h, DK : 2 * DK, :].astype(f32)
            tail = got[i, h, 2 * DK : 2 * DK + EXTRA, :].astype(f32)
            a = tail[0:1] + tail[EXTRA // 2 : EXTRA // 2 + 1]
            both = mm(m, jnp.concatenate([fades[h] * eye - maps[h], states[h]], axis=1))
            maps[h] = a * maps[h] + both[:, :DK]
            states[h] = a * states[h] - both[:, DK:] + s
            fades[h] = a * fades[h]

    @pl.when(first)
    def _():
        for h in range(hb):
            start[h] = jnp.zeros((DK, DV), bf16)

    chain = pltpu.make_async_remote_copy(
        src_ref=ready,
        dst_ref=start,
        send_sem=chain_send,
        recv_sem=chain_recv,
        device_id=at((me + n1) % (n1 * n2)),
        device_id_type=MESH,
    )

    @pl.when(jnp.logical_not(first))
    def _():
        chain.wait_recv()

    @pl.when(jnp.logical_not(last))
    def _():
        for h in range(hb):
            begin = start[h]
            ready[h] = (
                fades[h] * begin.astype(f32) - mm(maps[h], begin) + states[h]
            ).astype(bf16)
        chain.start()

    returned = []
    for i in range(n1):
        for h in range(hb):
            begin = start[h]
            back[i, h] = (
                pre_a[i, h, 0:1] * begin.astype(f32) - mm(pre_m[i, h], begin) + pre_s[i, h]
            ).astype(bf16)

    mine = pl.ds(place * hb, hb)
    for d in range(1, n1):
        peer = (place + d) % n1
        copy = pltpu.make_async_remote_copy(
            src_ref=back.at[peer],
            dst_ref=out_ref.at[mine],
            send_sem=back_send.at[d],
            recv_sem=back_recv.at[place],
            device_id=at(base + peer),
            device_id_type=MESH,
        )
        copy.start()
        returned.append(copy)
    kept = pltpu.make_async_copy(back.at[place], out_ref.at[mine], back_recv.at[place])
    kept.start()
    for i in range(n1):
        part = out_ref.at[pl.ds(i * hb, hb)]
        pltpu.make_async_copy(part, part, back_recv.at[i]).wait()
    for copy in outgoing + returned:
        copy.wait_send()

    @pl.when(jnp.logical_not(last))
    def _():
        chain.wait_send()


def carried_in(msg, n_ctx):
    heads = msg.shape[0]
    n1 = math.gcd(math.gcd(heads, n_ctx), 8)
    n2 = n_ctx // n1
    hb = heads // n1
    return pl.pallas_call(
        functools.partial(carry_kernel, n1, n2, hb),
        in_specs=[pl.BlockSpec(memory_space=pltpu.VMEM)],
        out_specs=pl.BlockSpec(memory_space=pltpu.VMEM),
        out_shape=jax.ShapeDtypeStruct((heads, DK, DV), bf16),
        scratch_shapes=[
            pltpu.VMEM((n1, hb, 2 * DK + EXTRA, DV), bf16),
            pltpu.VMEM((n1, hb, DK, DK), bf16),
            pltpu.VMEM((n1, hb, DK, DV), f32),
            pltpu.VMEM((n1, hb, 8, DV), f32),
            pltpu.VMEM((hb, DK, DV), bf16),
            pltpu.VMEM((hb, DK, DV), bf16),
            pltpu.VMEM((n1, hb, DK, DV), bf16),
            pltpu.SemaphoreType.DMA((n1,)),
            pltpu.SemaphoreType.DMA((n1,)),
            pltpu.SemaphoreType.DMA,
            pltpu.SemaphoreType.DMA,
            pltpu.SemaphoreType.DMA((n1,)),
            pltpu.SemaphoreType.DMA((n1,)),
        ],
        compiler_params=pltpu.CompilerParams(
            collective_id=0, has_side_effects=True, vmem_limit_bytes=48 << 20
        ),
        name="carried_in",
    )(msg)


def finish_kernel(heads, emit_ref, probe_ref, start_ref, gate_ref, gain_ref, weight_ref, out_ref, acc):
    step = pl.program_id(0)
    parts = []
    for h in range(heads):
        lo, hi = h * DV, (h + 1) * DV
        core = emit_ref[:, lo:hi] + mm(probe_ref[:, h * DK : (h + 1) * DK], start_ref[h])
        scale = lax.rsqrt(jnp.mean(core * core, axis=-1, keepdims=True) + 1e-06)
        gate = gate_ref[:, lo:hi].astype(f32)
        parts.append((core * scale * gain_ref[...] * silu(gate)).astype(bf16))
    part = jnp.dot(jnp.concatenate(parts, axis=1), weight_ref[...], preferred_element_type=f32)

    @pl.when(step == 0)
    def _():
        acc[...] = part

    @pl.when(step > 0)
    def _():
        acc[...] += part

    @pl.when(step == pl.num_programs(0) - 1)
    def _():
        out_ref[...] = acc[...].astype(bf16)


def finish(emitted, probes, starting, gate_values, norm_gain, out_weight):
    rows = emitted.shape[0]
    value_heads = starting.shape[0]
    heads = math.gcd(value_heads, 4)
    width = out_weight.shape[1]
    wide = lambda n: pl.BlockSpec((rows, n), lambda g: (0, g))
    return pl.pallas_call(
        functools.partial(finish_kernel, heads),
        grid=(value_heads // heads,),
        in_specs=[
            wide(heads * DV), wide(heads * DK),
            pl.BlockSpec((heads, DK, DV), lambda g: (g, 0, 0)),
            wide(heads * DV),
            pl.BlockSpec((1, DV), lambda g: (0, 0)),
            pl.BlockSpec((heads * DV, width), lambda g: (g, 0)),
        ],
        out_specs=pl.BlockSpec((rows, width), lambda g: (0, 0)),
        out_shape=jax.ShapeDtypeStruct((rows, width), bf16),
        scratch_shapes=[pltpu.VMEM((rows, width), f32)],
        compiler_params=pltpu.CompilerParams(vmem_limit_bytes=56 << 20),
        name="finish",
    )(emitted, probes, starting, gate_values, norm_gain.reshape(1, DV), out_weight)


def local(
    n_ctx, n_tp,
    query_in, key_in, value_in, gate_values, query_conv, key_conv, value_conv,
    beta_rate, log_decay, norm_gain, out_weight,
):
    edge = query_conv.shape[0] - 1
    row_count = query_in.shape[0]
    tails = [a[row_count - edge :] for a in (query_in, key_in, value_in)]
    rim = lax.ppermute(
        jnp.concatenate(tails, axis=1), "ctx", [(i, i + 1) for i in range(n_ctx - 1)]
    )
    rim = jnp.pad(rim.astype(f32), ((PAD - edge, 0), (0, 0)))
    q_cols, k_cols = query_in.shape[1], key_in.shape[1]
    rims = (rim[:, :q_cols], rim[:, q_cols : q_cols + k_cols], rim[:, q_cols + k_cols :])
    taps = tuple(a.astype(f32) for a in (query_conv, key_conv, value_conv))
    cum = jnp.cumsum(log_decay, axis=1)
    emitted, probes, msg = local_maps(query_in, key_in, value_in, rims, taps, cum, beta_rate)
    starting = carried_in(msg, n_ctx)
    partial = finish(emitted, probes, starting, gate_values, norm_gain, out_weight)
    if n_tp == 1:
        return partial
    return lax.psum_scatter(partial, "tp", scatter_dimension=0, tiled=True)


def solution(mesh):
    return jax.shard_map(
        functools.partial(local, mesh.shape["ctx"], mesh.shape["tp"]),
        mesh=mesh,
        in_specs=(
            P("ctx", "tp"), P("ctx", "tp"), P("ctx", "tp"), P("ctx", "tp"),
            P(None, "tp"), P(None, "tp"), P(None, "tp"),
            P("tp", "ctx"), P("tp", "ctx"), P(), P("tp", None),
        ),
        out_specs=P(("ctx", "tp"), None),
        check_vma=False,
    )
```

```python
import functools
import math

import jax
import jax.numpy as jnp
from jax import lax
from jax.experimental import pallas as pl
from jax.experimental.pallas import tpu as pltpu
from jax.sharding import PartitionSpec as P

HK = 16
HV = 32
DK = 128
DV = 128
SUB = 128
RIM = 16
EXTRA = 16
MESH = pl.DeviceIdType.MESH
f32 = jnp.float32
bf16 = jnp.bfloat16


def mm(a, b):
    return jnp.dot(a.astype(bf16), b.astype(bf16), preferred_element_type=f32)


def split(a):
    high = a.astype(bf16)
    return high, (a - high.astype(f32)).astype(bf16)


def silu(x):
    return x / (1.0 + jnp.exp(-x))


def conv(raw_ref, rim, taps_ref, lo, hi):
    rows = raw_ref.shape[0]
    joined = jnp.concatenate([rim[RIM // 2 :, lo:hi], raw_ref[:, lo:hi].astype(f32)], axis=0)
    taps = taps_ref[:, lo:hi].astype(f32)
    count = taps.shape[0]
    first = RIM // 2 - count + 1
    total = taps[0:1] * joined[first : first + rows]
    for j in range(1, count):
        total = total + taps[j : j + 1] * joined[first + j : first + j + rows]
    return silu(total)


def running_sums(decay):
    rows = decay.shape[1]
    row = lax.broadcasted_iota(jnp.int32, (rows, rows), 0)
    col = lax.broadcasted_iota(jnp.int32, (rows, rows), 1)
    ones = (row <= col).astype(f32).astype(bf16)
    high, rest = split(decay)
    middle, low = split(decay - high.astype(f32))
    return mm(high, ones) + (mm(middle, ones) + mm(low, ones))


def unit_lower_inverses(lowers):
    size = lowers[0].shape[0]
    row = lax.broadcasted_iota(jnp.int32, (size, size), 0)
    col = lax.broadcasted_iota(jnp.int32, (size, size), 1)
    eye = (row == col).astype(f32)
    pair = ((row // 2) == (col // 2)) & (row != col)
    found = [eye - jnp.where(pair, low, 0.0) for low in lowers]
    step = 2
    while step < size:
        take = ((row // (2 * step)) == (col // (2 * step))) & ((row // step) != (col // step))
        halves = [x.astype(bf16) for x in found]
        first = [mm(jnp.where(take, low, 0.0), x) for low, x in zip(lowers, halves)]
        found = [f - mm(x, y) for f, x, y in zip(found, halves, first)]
        step *= 2
    return [x.astype(bf16) for x in found]


def layer_kernel(
    n1, n2, key_heads, ratio, hb,
    q_ref, k_ref, v_ref, qtap, ktap, vtap, beta_ref, decay_ref, gain_ref,
    q_hbm, k_hbm, v_hbm, gate_hbm, weight_hbm, out_ref,
    rates, rim, gate, weight, emitted, probing, msg, got, pre_m, pre_s, pre_a, start, ready, back, starting, gated,
    rim_send, rim_recv, load_sem, send_sem, recv_sem, chain_send, chain_recv, back_send, back_recv,
):
    step = pl.program_id(0)
    steps = pl.num_programs(0)
    me = lax.axis_index("ctx")
    tp = lax.axis_index("tp")
    total_devices = n1 * n2
    plane = me // n1
    place = me % n1
    base = plane * n1
    first, last = plane == 0, plane == n2 - 1
    rows = q_ref.shape[0]
    q_cols, v_cols = q_hbm.shape[1], v_hbm.shape[1]
    heads = key_heads * ratio
    per_step = heads // hb

    def at(index):
        return (index, tp)

    rim_cols = ((q_hbm, 0, q_cols), (k_hbm, q_cols, q_cols), (v_hbm, 2 * q_cols, v_cols))
    rim_copies = [
        pltpu.make_async_remote_copy(
            src_ref=source.at[pl.ds(rows - RIM, RIM)],
            dst_ref=rim.at[:, pl.ds(offset, width)],
            send_sem=rim_send.at[i],
            recv_sem=rim_recv.at[i],
            device_id=at((me + 1) % total_devices),
            device_id_type=MESH,
        )
        for i, (source, offset, width) in enumerate(rim_cols)
    ]
    weight_copy = pltpu.make_async_copy(weight_hbm, weight, load_sem.at[0])
    gate_copy = pltpu.make_async_copy(gate_hbm, gate, load_sem.at[1])

    @pl.when(step == 0)
    def _():
        barrier = pltpu.get_barrier_semaphore()

        def greet(index):
            pl.semaphore_signal(barrier, inc=1, device_id=at(index), device_id_type=MESH)

        partners = n1 - 1 + jnp.where(first, 0, 1) + jnp.where(last, 0, 1)
        for d in range(1, n1):
            greet(base + (place + d) % n1)

        @pl.when(jnp.logical_not(first))
        def _():
            greet(me - n1)

        @pl.when(jnp.logical_not(last))
        def _():
            greet(me + n1)

        if n1 > 1:
            before = jnp.logical_and(place == 0, me > 0)
            after = jnp.logical_and(place == n1 - 1, me < total_devices - 1)
            partners = partners + jnp.where(before, 1, 0) + jnp.where(after, 1, 0)

            @pl.when(before)
            def _():
                greet(me - 1)

            @pl.when(after)
            def _():
                greet(me + 1)

        pl.semaphore_wait(barrier, partners)

        @pl.when(me < total_devices - 1)
        def _():
            for copy in rim_copies:
                copy.start()

        gate_copy.start()
        weight_copy.start()
        sums = running_sums(decay_ref[...])
        for g in range(rates.shape[0]):
            rates[g, 0:heads] = sums[g * heads : (g + 1) * heads]
            rates[g, heads : 2 * heads] = beta_ref[g * heads : (g + 1) * heads, :]

        @pl.when(me == 0)
        def _():
            rim[...] = jnp.zeros_like(rim)

        @pl.when(me > 0)
        def _():
            for copy in rim_copies:
                copy.wait_recv()

    local_rates = rates[step]
    rate_cols = local_rates.T
    key_width, value_width = key_heads * DK, heads * DV

    def rim_part(offset, width):
        return rim[:, pl.ds(pl.multiple_of(offset + step * width, DK), width)].astype(f32)

    q_rim = rim_part(0, key_width)
    k_rim = rim_part(q_cols, key_width)
    v_rim = rim_part(2 * q_cols, value_width)
    row = lax.broadcasted_iota(jnp.int32, (rows, rows), 0)
    col = lax.broadcasted_iota(jnp.int32, (rows, rows), 1)
    sub = min(SUB, rows)
    count = rows // sub
    lowers, sims, rights, probes, tails, totals = [], [], [], [], [], []
    for g in range(key_heads):
        lo, hi = g * DK, (g + 1) * DK
        q = conv(q_ref, q_rim, qtap, lo, hi)
        k = conv(k_ref, k_rim, ktap, lo, hi)
        k = k * lax.rsqrt(jnp.sum(k * k, axis=-1, keepdims=True) + 1e-06)
        k_turned = k.T
        k_right = k_turned.astype(bf16)
        kk = mm(k, k_right)
        qk = mm(q, k_right)
        for r in range(ratio):
            h = g * ratio + r
            v = conv(v_ref, v_rim, vtap, h * DV, (h + 1) * DV)
            cum = rate_cols[:, h : h + 1]
            beta = rate_cols[:, heads + h : heads + h + 1]
            cum_row = local_rates[h : h + 1]
            fade = jnp.exp(jnp.minimum(cum - cum_row, 0.0))
            lowers.append(jnp.where(row > col, beta * fade * kk, 0.0))
            sims.append(jnp.where(row >= col, fade * qk, 0.0).astype(bf16))
            grown = jnp.exp(cum)
            rights.append(jnp.concatenate([beta * v, (beta * grown) * k], axis=1))
            probes.append(grown * q)
            end = cum_row[:, rows - 1 : rows]
            tails.append((k_turned * jnp.exp(end - cum_row)).astype(bf16))
            totals.append(jnp.exp(end))
    pieces = [
        low[i * sub : (i + 1) * sub, i * sub : (i + 1) * sub] for low in lowers for i in range(count)
    ]
    inverses = unit_lower_inverses(pieces)
    upper = lax.broadcasted_iota(jnp.int32, (EXTRA, DV), 0) < EXTRA // 2
    for h in range(heads):
        low = lowers[h]
        solved = []
        for i in range(count):
            right = rights[h][i * sub : (i + 1) * sub]
            if i > 0:
                before = jnp.concatenate(solved, axis=0)
                right = right - mm(low[i * sub : (i + 1) * sub, : i * sub], before)
            solved.append(mm(inverses[h * count + i], right).astype(bf16))
        solved = jnp.concatenate(solved, axis=0)
        seen = mm(sims[h], solved)
        lanes = pl.ds(pl.multiple_of((step * heads + h) * DV, DV), DV)
        emitted[:, lanes] = seen[:, :DV]
        probing[:, lanes] = (probes[h] - seen[:, DV:]).astype(bf16)
        update = mm(tails[h], solved)
        at_head = step * heads + h
        msg[at_head, 0:DK, :] = update[:, DV:].astype(bf16)
        msg[at_head, DK : 2 * DK, :] = update[:, :DV].astype(bf16)
        high, rest = split(jnp.broadcast_to(totals[h], (EXTRA, DV)))
        msg[at_head, 2 * DK :, :] = jnp.where(upper, high.astype(f32), rest.astype(f32)).astype(bf16)

    def map_copy(peer):
        return pltpu.make_async_remote_copy(
            src_ref=msg.at[pl.ds(peer * hb, hb)],
            dst_ref=got.at[place],
            send_sem=send_sem.at[peer],
            recv_sem=recv_sem.at[place],
            device_id=at(base + peer),
            device_id_type=MESH,
        )

    for j in range(per_step):
        peer = step * per_step + j

        @pl.when(peer != place)
        def _():
            map_copy(peer).start()

        @pl.when(peer == place)
        def _():
            pltpu.make_async_copy(
                msg.at[pl.ds(peer * hb, hb)], got.at[place], recv_sem.at[place]
            ).start()

    @pl.when(step == steps - 1)
    def _():
        maps = [jnp.zeros((DK, DK), f32) for _ in range(hb)]
        states = [jnp.zeros((DK, DV), f32) for _ in range(hb)]
        fades = [jnp.ones((1, DV), f32) for _ in range(hb)]
        eye_row = lax.broadcasted_iota(jnp.int32, (DK, DK), 0)
        eye_col = lax.broadcasted_iota(jnp.int32, (DK, DK), 1)
        eye = (eye_row == eye_col).astype(f32)
        for i in range(n1):
            pltpu.make_async_copy(got.at[i], got.at[i], recv_sem.at[i]).wait()
            for h in range(hb):
                pre_m[i, h] = maps[h].astype(bf16)
                pre_s[i, h] = states[h]
                pre_a[i, h] = jnp.broadcast_to(fades[h], (8, DV))
                m = got[i, h, 0:DK, :]
                s = got[i, h, DK : 2 * DK, :].astype(f32)
                tail = got[i, h, 2 * DK : 2 * DK + EXTRA, :].astype(f32)
                a = tail[0:1] + tail[EXTRA // 2 : EXTRA // 2 + 1]
                both = mm(m, jnp.concatenate([fades[h] * eye - maps[h], states[h]], axis=1))
                maps[h] = a * maps[h] + both[:, :DK]
                states[h] = a * states[h] - both[:, DK:] + s
                fades[h] = a * fades[h]

        @pl.when(first)
        def _():
            for h in range(hb):
                start[h] = jnp.zeros((DK, DV), bf16)

        chain = pltpu.make_async_remote_copy(
            src_ref=ready,
            dst_ref=start,
            send_sem=chain_send,
            recv_sem=chain_recv,
            device_id=at((me + n1) % total_devices),
            device_id_type=MESH,
        )

        @pl.when(jnp.logical_not(first))
        def _():
            chain.wait_recv()

        @pl.when(jnp.logical_not(last))
        def _():
            for h in range(hb):
                begin = start[h]
                ready[h] = (
                    fades[h] * begin.astype(f32) - mm(maps[h], begin) + states[h]
                ).astype(bf16)
            chain.start()

        for i in range(n1):
            for h in range(hb):
                begin = start[h]
                back[i, h] = (
                    pre_a[i, h, 0:1] * begin.astype(f32) - mm(pre_m[i, h], begin) + pre_s[i, h]
                ).astype(bf16)

        mine = pl.ds(place * hb, hb)
        returned = []
        for d in range(1, n1):
            peer = (place + d) % n1
            copy = pltpu.make_async_remote_copy(
                src_ref=back.at[peer],
                dst_ref=starting.at[mine],
                send_sem=back_send.at[d],
                recv_sem=back_recv.at[place],
                device_id=at(base + peer),
                device_id_type=MESH,
            )
            copy.start()
            returned.append(copy)
        pltpu.make_async_copy(back.at[place], starting.at[mine], back_recv.at[place]).start()
        gate_copy.wait()
        gain = gain_ref[...]
        for i in range(n1):
            part = starting.at[pl.ds(i * hb, hb)]
            pltpu.make_async_copy(part, part, back_recv.at[i]).wait()
            for h in range(i * hb, (i + 1) * hb):
                lo, hi = h * DV, (h + 1) * DV
                core = emitted[:, lo:hi] + mm(probing[:, lo:hi], starting[h])
                scale = lax.rsqrt(jnp.mean(core * core, axis=-1, keepdims=True) + 1e-06)
                gated[:, lo:hi] = (
                    core * scale * gain * silu(gate[:, lo:hi].astype(f32))
                ).astype(bf16)
        weight_copy.wait()
        width = out_ref.shape[1]
        tile = math.gcd(width, 512)

        def project(t, carry):
            lanes = pl.ds(pl.multiple_of(t * tile, tile), tile)
            out_ref[:, lanes] = jnp.dot(
                gated[...], weight[:, lanes], preferred_element_type=f32
            ).astype(bf16)
            return carry

        lax.fori_loop(0, width // tile, project, 0)
        for copy in returned:
            copy.wait_send()
        for peer in range(n1):
            @pl.when(peer != place)
            def _():
                map_copy(peer).wait_send()

        @pl.when(jnp.logical_not(last))
        def _():
            chain.wait_send()

        @pl.when(me < total_devices - 1)
        def _():
            for copy in rim_copies:
                copy.wait_send()


def layer(n_ctx, query, key, value, gate, taps, beta, decay, gain, weight):
    rows, q_cols = query.shape
    v_cols = value.shape[1]
    key_heads, value_heads = q_cols // DK, v_cols // DV
    ratio = value_heads // key_heads
    n1 = math.gcd(math.gcd(value_heads, n_ctx), 8)
    n2 = n_ctx // n1
    hb = value_heads // n1
    step = math.gcd(key_heads, 2)
    while (step * ratio) % hb:
        step *= 2
    groups = key_heads // step
    heads = step * ratio
    kw, vw = step * DK, heads * DV
    width = weight.shape[1]
    wide = lambda n, size: pl.BlockSpec((n, size), lambda g: (0, g))
    whole = lambda shape: pl.BlockSpec(shape, lambda g: (0, 0))
    anywhere = pl.BlockSpec(memory_space=pl.ANY)
    count = taps[0].shape[0]
    return pl.pallas_call(
        functools.partial(layer_kernel, n1, n2, step, ratio, hb),
        grid=(groups,),
        in_specs=[
            wide(rows, kw), wide(rows, kw), wide(rows, vw),
            wide(count, kw), wide(count, kw), wide(count, vw),
            whole(beta.shape), whole(decay.shape), whole((1, DV)),
            anywhere, anywhere, anywhere, anywhere, anywhere,
        ],
        out_specs=whole((rows, width)),
        out_shape=jax.ShapeDtypeStruct((rows, width), bf16),
        scratch_shapes=[
            pltpu.VMEM((groups, 2 * heads, rows), f32),
            pltpu.VMEM((RIM, 2 * q_cols + v_cols), bf16),
            pltpu.VMEM(gate.shape, bf16),
            pltpu.VMEM(weight.shape, bf16),
            pltpu.VMEM((rows, v_cols), f32),
            pltpu.VMEM((rows, v_cols), bf16),
            pltpu.VMEM((value_heads, 2 * DK + EXTRA, DV), bf16),
            pltpu.VMEM((n1, hb, 2 * DK + EXTRA, DV), bf16),
            pltpu.VMEM((n1, hb, DK, DK), bf16),
            pltpu.VMEM((n1, hb, DK, DV), f32),
            pltpu.VMEM((n1, hb, 8, DV), f32),
            pltpu.VMEM((hb, DK, DV), bf16),
            pltpu.VMEM((hb, DK, DV), bf16),
            pltpu.VMEM((n1, hb, DK, DV), bf16),
            pltpu.VMEM((value_heads, DK, DV), bf16),
            pltpu.VMEM((rows, v_cols), bf16),
            pltpu.SemaphoreType.DMA((3,)),
            pltpu.SemaphoreType.DMA((3,)),
            pltpu.SemaphoreType.DMA((2,)),
            pltpu.SemaphoreType.DMA((n1,)),
            pltpu.SemaphoreType.DMA((n1,)),
            pltpu.SemaphoreType.DMA,
            pltpu.SemaphoreType.DMA,
            pltpu.SemaphoreType.DMA((n1,)),
            pltpu.SemaphoreType.DMA((n1,)),
        ],
        compiler_params=pltpu.CompilerParams(
            collective_id=0, has_side_effects=True, vmem_limit_bytes=60 << 20
        ),
        name="layer",
    )(
        query, key, value, *taps, beta, decay, gain.reshape(1, DV),
        query, key, value, gate, weight,
    )


def local(
    n_ctx, n_tp,
    query_in, key_in, value_in, gate_values, query_conv, key_conv, value_conv,
    beta_rate, log_decay, norm_gain, out_weight,
):
    partial = layer(
        n_ctx, query_in, key_in, value_in, gate_values, (query_conv, key_conv, value_conv),
        beta_rate, log_decay, norm_gain, out_weight,
    )
    if n_tp == 1:
        return partial
    return lax.psum_scatter(partial, "tp", scatter_dimension=0, tiled=True)


def solution(mesh):
    return jax.shard_map(
        functools.partial(local, mesh.shape["ctx"], mesh.shape["tp"]),
        mesh=mesh,
        in_specs=(
            P("ctx", "tp"), P("ctx", "tp"), P("ctx", "tp"), P("ctx", "tp"),
            P(None, "tp"), P(None, "tp"), P(None, "tp"),
            P("tp", "ctx"), P("tp", "ctx"), P(), P("tp", None),
        ),
        out_specs=P(("ctx", "tp"), None),
        check_vma=False,
    )
```

```python
import functools
import math

import jax
import jax.numpy as jnp
from jax import lax
from jax.experimental import pallas as pl
from jax.experimental.pallas import tpu as pltpu
from jax.sharding import PartitionSpec as P

HK = 16
HV = 32
DK = 128
DV = 128
SUB = 128
RIM = 16
EXTRA = 16
MESH = pl.DeviceIdType.MESH
f32 = jnp.float32
bf16 = jnp.bfloat16


def mm(a, b):
    return jnp.dot(a.astype(bf16), b.astype(bf16), preferred_element_type=f32)


def split(a):
    high = a.astype(bf16)
    return high, (a - high.astype(f32)).astype(bf16)


def silu(x):
    return x / (1.0 + jnp.exp(-x))


def conv(raw_ref, rim, taps_ref, lo, hi):
    rows = raw_ref.shape[0]
    joined = jnp.concatenate([rim[RIM // 2 :, lo:hi], raw_ref[:, lo:hi].astype(f32)], axis=0)
    taps = taps_ref[:, lo:hi].astype(f32)
    count = taps.shape[0]
    first = RIM // 2 - count + 1
    total = taps[0:1] * joined[first : first + rows]
    for j in range(1, count):
        total = total + taps[j : j + 1] * joined[first + j : first + j + rows]
    return silu(total)


def running_sums(decay):
    rows = decay.shape[1]
    row = lax.broadcasted_iota(jnp.int32, (rows, rows), 0)
    col = lax.broadcasted_iota(jnp.int32, (rows, rows), 1)
    ones = (row <= col).astype(f32).astype(bf16)
    high, rest = split(decay)
    middle, low = split(decay - high.astype(f32))
    return mm(high, ones) + (mm(middle, ones) + mm(low, ones))


def unit_lower_inverses(lowers):
    size = lowers[0].shape[0]
    row = lax.broadcasted_iota(jnp.int32, (size, size), 0)
    col = lax.broadcasted_iota(jnp.int32, (size, size), 1)
    eye = (row == col).astype(f32)
    pair = ((row // 2) == (col // 2)) & (row != col)
    found = [eye - jnp.where(pair, low, 0.0) for low in lowers]
    step = 2
    while step < size:
        take = ((row // (2 * step)) == (col // (2 * step))) & ((row // step) != (col // step))
        halves = [x.astype(bf16) for x in found]
        first = [mm(jnp.where(take, low, 0.0), x) for low, x in zip(lowers, halves)]
        found = [f - mm(x, y) for f, x, y in zip(found, halves, first)]
        step *= 2
    return [x.astype(bf16) for x in found]


def layer_kernel(
    n1, n2, key_heads, ratio, hb,
    q_ref, k_ref, v_ref, qtap, ktap, vtap, beta_ref, decay_ref, gain_ref,
    q_hbm, k_hbm, v_hbm, gate_hbm, weight_hbm, out_ref,
    rates, rim, gate, weight, emitted, probing, msg, got, pre_m, pre_s, pre_a, start, ready, back, starting, gated, acc,
    rim_send, rim_recv, load_sem, send_sem, recv_sem, chain_send, chain_recv, back_send, back_recv,
):
    step = pl.program_id(0)
    steps = pl.num_programs(0)
    me = lax.axis_index("ctx")
    tp = lax.axis_index("tp")
    total_devices = n1 * n2
    plane = me // n1
    place = me % n1
    base = plane * n1
    first, last = plane == 0, plane == n2 - 1
    rows = q_ref.shape[0]
    q_cols, v_cols = q_hbm.shape[1], v_hbm.shape[1]
    heads = key_heads * ratio
    per_step = heads // hb

    def at(index):
        return (index, tp)

    rim_cols = ((q_hbm, 0, q_cols), (k_hbm, q_cols, q_cols), (v_hbm, 2 * q_cols, v_cols))
    rim_copies = [
        pltpu.make_async_remote_copy(
            src_ref=source.at[pl.ds(rows - RIM, RIM)],
            dst_ref=rim.at[:, pl.ds(offset, width)],
            send_sem=rim_send.at[i],
            recv_sem=rim_recv.at[i],
            device_id=at((me + 1) % total_devices),
            device_id_type=MESH,
        )
        for i, (source, offset, width) in enumerate(rim_cols)
    ]
    weight_copy = pltpu.make_async_copy(weight_hbm, weight, load_sem.at[0])
    gate_copy = pltpu.make_async_copy(gate_hbm, gate, load_sem.at[1])

    @pl.when(step == 0)
    def _():
        barrier = pltpu.get_barrier_semaphore()

        def greet(index):
            pl.semaphore_signal(barrier, inc=1, device_id=at(index), device_id_type=MESH)

        partners = n1 - 1 + jnp.where(first, 0, 1) + jnp.where(last, 0, 1)
        for d in range(1, n1):
            greet(base + (place + d) % n1)

        @pl.when(jnp.logical_not(first))
        def _():
            greet(me - n1)

        @pl.when(jnp.logical_not(last))
        def _():
            greet(me + n1)

        if n1 > 1:
            before = jnp.logical_and(place == 0, me > 0)
            after = jnp.logical_and(place == n1 - 1, me < total_devices - 1)
            partners = partners + jnp.where(before, 1, 0) + jnp.where(after, 1, 0)

            @pl.when(before)
            def _():
                greet(me - 1)

            @pl.when(after)
            def _():
                greet(me + 1)

        pl.semaphore_wait(barrier, partners)

        @pl.when(me < total_devices - 1)
        def _():
            for copy in rim_copies:
                copy.start()

        gate_copy.start()
        weight_copy.start()
        sums = running_sums(decay_ref[...])
        for g in range(rates.shape[0]):
            rates[g, 0:heads] = sums[g * heads : (g + 1) * heads]
            rates[g, heads : 2 * heads] = beta_ref[g * heads : (g + 1) * heads, :]

        @pl.when(me == 0)
        def _():
            rim[...] = jnp.zeros_like(rim)

        @pl.when(me > 0)
        def _():
            for copy in rim_copies:
                copy.wait_recv()

    local_rates = rates[step]
    rate_cols = local_rates.T
    key_width, value_width = key_heads * DK, heads * DV

    def rim_part(offset, width):
        return rim[:, pl.ds(pl.multiple_of(offset + step * width, DK), width)].astype(f32)

    q_rim = rim_part(0, key_width)
    k_rim = rim_part(q_cols, key_width)
    v_rim = rim_part(2 * q_cols, value_width)
    row = lax.broadcasted_iota(jnp.int32, (rows, rows), 0)
    col = lax.broadcasted_iota(jnp.int32, (rows, rows), 1)
    sub = min(SUB, rows)
    count = rows // sub
    lowers, sims, rights, probes, tails, totals = [], [], [], [], [], []
    for g in range(key_heads):
        lo, hi = g * DK, (g + 1) * DK
        q = conv(q_ref, q_rim, qtap, lo, hi)
        k = conv(k_ref, k_rim, ktap, lo, hi)
        k = k * lax.rsqrt(jnp.sum(k * k, axis=-1, keepdims=True) + 1e-06)
        k_turned = k.T
        k_right = k_turned.astype(bf16)
        kk = mm(k, k_right)
        qk = mm(q, k_right)
        for r in range(ratio):
            h = g * ratio + r
            v = conv(v_ref, v_rim, vtap, h * DV, (h + 1) * DV)
            cum = rate_cols[:, h : h + 1]
            beta = rate_cols[:, heads + h : heads + h + 1]
            cum_row = local_rates[h : h + 1]
            fade = jnp.exp(jnp.minimum(cum - cum_row, 0.0))
            lowers.append(jnp.where(row > col, beta * fade * kk, 0.0))
            sims.append(jnp.where(row >= col, fade * qk, 0.0).astype(bf16))
            grown = jnp.exp(cum)
            rights.append(jnp.concatenate([beta * v, (beta * grown) * k], axis=1))
            probes.append(grown * q)
            end = cum_row[:, rows - 1 : rows]
            tails.append((k_turned * jnp.exp(end - cum_row)).astype(bf16))
            totals.append(jnp.exp(end))
    pieces = [
        low[i * sub : (i + 1) * sub, i * sub : (i + 1) * sub] for low in lowers for i in range(count)
    ]
    inverses = unit_lower_inverses(pieces)
    upper = lax.broadcasted_iota(jnp.int32, (EXTRA, DV), 0) < EXTRA // 2
    for h in range(heads):
        low = lowers[h]
        solved = []
        for i in range(count):
            right = rights[h][i * sub : (i + 1) * sub]
            if i > 0:
                before = jnp.concatenate(solved, axis=0)
                right = right - mm(low[i * sub : (i + 1) * sub, : i * sub], before)
            solved.append(mm(inverses[h * count + i], right).astype(bf16))
        solved = jnp.concatenate(solved, axis=0)
        seen = mm(sims[h], solved)
        lanes = pl.ds(pl.multiple_of((step * heads + h) * DV, DV), DV)
        emitted[:, lanes] = seen[:, :DV]
        probing[:, lanes] = (probes[h] - seen[:, DV:]).astype(bf16)
        update = mm(tails[h], solved)
        at_head = step * heads + h
        msg[at_head, 0:DK, :] = update[:, DV:].astype(bf16)
        msg[at_head, DK : 2 * DK, :] = update[:, :DV].astype(bf16)
        high, rest = split(jnp.broadcast_to(totals[h], (EXTRA, DV)))
        msg[at_head, 2 * DK :, :] = jnp.where(upper, high.astype(f32), rest.astype(f32)).astype(bf16)

    def map_copy(peer):
        return pltpu.make_async_remote_copy(
            src_ref=msg.at[pl.ds(peer * hb, hb)],
            dst_ref=got.at[place],
            send_sem=send_sem.at[peer],
            recv_sem=recv_sem.at[place],
            device_id=at(base + peer),
            device_id_type=MESH,
        )

    for j in range(per_step):
        peer = step * per_step + j

        @pl.when(peer != place)
        def _():
            map_copy(peer).start()

        @pl.when(peer == place)
        def _():
            pltpu.make_async_copy(
                msg.at[pl.ds(peer * hb, hb)], got.at[place], recv_sem.at[place]
            ).start()

    turn = jnp.minimum(place // per_step + 2 + plane, steps - 1)
    late = jnp.logical_and(place == n1 - 1, 2 * plane >= n2)

    def chain_copy(h):
        return pltpu.make_async_remote_copy(
            src_ref=ready.at[h],
            dst_ref=start.at[h],
            send_sem=chain_send.at[h],
            recv_sem=chain_recv.at[h],
            device_id=at((me + n1) % total_devices),
            device_id_type=MESH,
        )

    def back_copy(d):
        return pltpu.make_async_remote_copy(
            src_ref=back.at[(place + d) % n1],
            dst_ref=starting.at[pl.ds(place * hb, hb)],
            send_sem=back_send.at[d],
            recv_sem=back_recv.at[place],
            device_id=at(base + (place + d) % n1),
            device_id_type=MESH,
        )

    def advance(i, h, begin):
        return (
            pre_a[i, h, 0:1] * begin.astype(f32) - mm(pre_m[i, h], begin) + pre_s[i, h]
        ).astype(bf16)

    def chain_and_return():
        @pl.when(first)
        def _():
            for h in range(hb):
                start[h] = jnp.zeros((DK, DV), bf16)

        for h in range(hb):
            @pl.when(jnp.logical_not(first))
            def _():
                chain_copy(h).wait_recv()

            @pl.when(jnp.logical_not(last))
            def _():
                ready[h] = advance(n1, h, start[h])
                chain_copy(h).start()

        for d in range(1, n1):
            peer = (place + d) % n1
            for h in range(hb):
                back[peer, h] = advance(peer, h, start[h])
            back_copy(d).start()
        for h in range(hb):
            back[place, h] = advance(place, h, start[h])
        pltpu.make_async_copy(
            back.at[place], starting.at[pl.ds(place * hb, hb)], back_recv.at[place]
        ).start()

    @pl.when(step == turn)
    def _():
        maps = [jnp.zeros((DK, DK), f32) for _ in range(hb)]
        states = [jnp.zeros((DK, DV), f32) for _ in range(hb)]
        fades = [jnp.ones((1, DV), f32) for _ in range(hb)]
        eye_row = lax.broadcasted_iota(jnp.int32, (DK, DK), 0)
        eye_col = lax.broadcasted_iota(jnp.int32, (DK, DK), 1)
        eye = (eye_row == eye_col).astype(f32)
        for i in range(n1 + 1):
            for h in range(hb):
                pre_m[i, h] = maps[h].astype(bf16)
                pre_s[i, h] = states[h]
                pre_a[i, h] = jnp.broadcast_to(fades[h], (8, DV))
            if i == n1:
                break
            pltpu.make_async_copy(got.at[i], got.at[i], recv_sem.at[i]).wait()
            for h in range(hb):
                m = got[i, h, 0:DK, :]
                s = got[i, h, DK : 2 * DK, :].astype(f32)
                tail = got[i, h, 2 * DK : 2 * DK + EXTRA, :].astype(f32)
                a = tail[0:1] + tail[EXTRA // 2 : EXTRA // 2 + 1]
                both = mm(m, jnp.concatenate([fades[h] * eye - maps[h], states[h]], axis=1))
                maps[h] = a * maps[h] + both[:, :DK]
                states[h] = a * states[h] - both[:, DK:] + s
                fades[h] = a * fades[h]

        @pl.when(jnp.logical_not(late))
        def _():
            chain_and_return()

    @pl.when(step == steps - 1)
    def _():
        gain = gain_ref[...]
        width = out_ref.shape[1]
        tile = math.gcd(width, 512)
        early = (n1 - 1) * hb * DV

        def gate_heads(i):
            part = starting.at[pl.ds(i * hb, hb)]
            pltpu.make_async_copy(part, part, back_recv.at[i]).wait()
            for h in range(i * hb, (i + 1) * hb):
                lo, hi = h * DV, (h + 1) * DV
                core = emitted[:, lo:hi] + mm(probing[:, lo:hi], starting[h])
                scale = lax.rsqrt(jnp.mean(core * core, axis=-1, keepdims=True) + 1e-06)
                gated[:, lo:hi] = (
                    core * scale * gain * silu(gate[:, lo:hi].astype(f32))
                ).astype(bf16)

        gate_copy.wait()
        for i in range(n1 - 1):
            gate_heads(i)

        @pl.when(late)
        def _():
            chain_and_return()

        weight_copy.wait()

        def project_early(t, carry):
            lanes = pl.ds(pl.multiple_of(t * tile, tile), tile)
            acc[:, lanes] = jnp.dot(
                gated[:, :early], weight[:early, lanes], preferred_element_type=f32
            )
            return carry

        def project_late(t, carry):
            lanes = pl.ds(pl.multiple_of(t * tile, tile), tile)
            total = jnp.dot(gated[:, early:], weight[early:, lanes], preferred_element_type=f32)
            if early > 0:
                total = total + acc[:, lanes]
            out_ref[:, lanes] = total.astype(bf16)
            return carry

        if early > 0:
            lax.fori_loop(0, width // tile, project_early, 0)
        gate_heads(n1 - 1)
        lax.fori_loop(0, width // tile, project_late, 0)
        for d in range(1, n1):
            back_copy(d).wait_send()
        for peer in range(n1):
            @pl.when(peer != place)
            def _():
                map_copy(peer).wait_send()

        @pl.when(jnp.logical_not(last))
        def _():
            for h in range(hb):
                chain_copy(h).wait_send()

        @pl.when(me < total_devices - 1)
        def _():
            for copy in rim_copies:
                copy.wait_send()


def layer(n_ctx, query, key, value, gate, taps, beta, decay, gain, weight):
    rows, q_cols = query.shape
    v_cols = value.shape[1]
    key_heads, value_heads = q_cols // DK, v_cols // DV
    ratio = value_heads // key_heads
    n1 = math.gcd(math.gcd(value_heads, n_ctx), 8)
    n2 = n_ctx // n1
    hb = value_heads // n1
    step = math.gcd(key_heads, 2)
    while (step * ratio) % hb:
        step *= 2
    groups = key_heads // step
    heads = step * ratio
    kw, vw = step * DK, heads * DV
    width = weight.shape[1]
    wide = lambda n, size: pl.BlockSpec((n, size), lambda g: (0, g))
    whole = lambda shape: pl.BlockSpec(shape, lambda g: (0, 0))
    anywhere = pl.BlockSpec(memory_space=pl.ANY)
    count = taps[0].shape[0]
    return pl.pallas_call(
        functools.partial(layer_kernel, n1, n2, step, ratio, hb),
        grid=(groups,),
        in_specs=[
            wide(rows, kw), wide(rows, kw), wide(rows, vw),
            wide(count, kw), wide(count, kw), wide(count, vw),
            whole(beta.shape), whole(decay.shape), whole((1, DV)),
            anywhere, anywhere, anywhere, anywhere, anywhere,
        ],
        out_specs=whole((rows, width)),
        out_shape=jax.ShapeDtypeStruct((rows, width), bf16),
        scratch_shapes=[
            pltpu.VMEM((groups, 2 * heads, rows), f32),
            pltpu.VMEM((RIM, 2 * q_cols + v_cols), bf16),
            pltpu.VMEM(gate.shape, bf16),
            pltpu.VMEM(weight.shape, bf16),
            pltpu.VMEM((rows, v_cols), f32),
            pltpu.VMEM((rows, v_cols), bf16),
            pltpu.VMEM((value_heads, 2 * DK + EXTRA, DV), bf16),
            pltpu.VMEM((n1, hb, 2 * DK + EXTRA, DV), bf16),
            pltpu.VMEM((n1 + 1, hb, DK, DK), bf16),
            pltpu.VMEM((n1 + 1, hb, DK, DV), f32),
            pltpu.VMEM((n1 + 1, hb, 8, DV), f32),
            pltpu.VMEM((hb, DK, DV), bf16),
            pltpu.VMEM((hb, DK, DV), bf16),
            pltpu.VMEM((n1, hb, DK, DV), bf16),
            pltpu.VMEM((value_heads, DK, DV), bf16),
            pltpu.VMEM((rows, v_cols), bf16),
            pltpu.VMEM((rows, width), f32),
            pltpu.SemaphoreType.DMA((3,)),
            pltpu.SemaphoreType.DMA((3,)),
            pltpu.SemaphoreType.DMA((2,)),
            pltpu.SemaphoreType.DMA((n1,)),
            pltpu.SemaphoreType.DMA((n1,)),
            pltpu.SemaphoreType.DMA((hb,)),
            pltpu.SemaphoreType.DMA((hb,)),
            pltpu.SemaphoreType.DMA((n1,)),
            pltpu.SemaphoreType.DMA((n1,)),
        ],
        compiler_params=pltpu.CompilerParams(
            collective_id=0, has_side_effects=True, vmem_limit_bytes=60 << 20
        ),
        name="layer",
    )(
        query, key, value, *taps, beta, decay, gain.reshape(1, DV),
        query, key, value, gate, weight,
    )


def local(
    n_ctx, n_tp,
    query_in, key_in, value_in, gate_values, query_conv, key_conv, value_conv,
    beta_rate, log_decay, norm_gain, out_weight,
):
    partial = layer(
        n_ctx, query_in, key_in, value_in, gate_values, (query_conv, key_conv, value_conv),
        beta_rate, log_decay, norm_gain, out_weight,
    )
    if n_tp == 1:
        return partial
    return lax.psum_scatter(partial, "tp", scatter_dimension=0, tiled=True)


def solution(mesh):
    return jax.shard_map(
        functools.partial(local, mesh.shape["ctx"], mesh.shape["tp"]),
        mesh=mesh,
        in_specs=(
            P("ctx", "tp"), P("ctx", "tp"), P("ctx", "tp"), P("ctx", "tp"),
            P(None, "tp"), P(None, "tp"), P(None, "tp"),
            P("tp", "ctx"), P("tp", "ctx"), P(), P("tp", None),
        ),
        out_specs=P(("ctx", "tp"), None),
        check_vma=False,
    )
```

```python
import functools
import math

import jax
import jax.numpy as jnp
from jax import lax
from jax.experimental import pallas as pl
from jax.experimental.pallas import tpu as pltpu
from jax.sharding import PartitionSpec as P

HK = 16
HV = 32
DK = 128
DV = 128
SUB = 128
RIM = 16
EXTRA = 16
MESH = pl.DeviceIdType.MESH
f32 = jnp.float32
bf16 = jnp.bfloat16


def mm(a, b):
    return jnp.dot(a.astype(bf16), b.astype(bf16), preferred_element_type=f32)


def split(a):
    high = a.astype(bf16)
    return high, (a - high.astype(f32)).astype(bf16)


def silu(x):
    return x / (1.0 + jnp.exp(-x))


def conv(raw_ref, rim, taps_ref, lo, hi):
    rows = raw_ref.shape[0]
    joined = jnp.concatenate([rim[RIM // 2 :, lo:hi], raw_ref[:, lo:hi].astype(f32)], axis=0)
    taps = taps_ref[:, lo:hi].astype(f32)
    count = taps.shape[0]
    first = RIM // 2 - count + 1
    total = taps[0:1] * joined[first : first + rows]
    for j in range(1, count):
        total = total + taps[j : j + 1] * joined[first + j : first + j + rows]
    return silu(total)


def running_sums(decay):
    rows = decay.shape[1]
    row = lax.broadcasted_iota(jnp.int32, (rows, rows), 0)
    col = lax.broadcasted_iota(jnp.int32, (rows, rows), 1)
    ones = (row <= col).astype(f32).astype(bf16)
    high, rest = split(decay)
    middle, low = split(decay - high.astype(f32))
    return mm(high, ones) + (mm(middle, ones) + mm(low, ones))


def odd_rows(x, step):
    count = x.shape[0] // (2 * step)
    return jnp.concatenate(
        [x[(2 * j + 1) * step : (2 * j + 2) * step] for j in range(count)], axis=0
    )


def with_odd_rows(even, odd, step):
    parts = []
    for j in range(odd.shape[0] // step):
        parts.append(even[2 * j * step : (2 * j + 1) * step])
        parts.append(odd[j * step : (j + 1) * step])
    return jnp.concatenate(parts, axis=0)


def unit_lower_inverses(lowers):
    size = lowers[0].shape[0]
    row = lax.broadcasted_iota(jnp.int32, (size, size), 0)
    col = lax.broadcasted_iota(jnp.int32, (size, size), 1)
    eye = (row == col).astype(f32)
    zero = jnp.zeros((size, size), f32)
    pair = ((row // 2) == (col // 2)) & (row != col)
    found = [eye - jnp.where(pair, low, 0.0) for low in lowers]
    step = 2
    while step < size:
        halves = [x.astype(bf16) for x in found]
        if step < 8:
            take = ((row // (2 * step)) == (col // (2 * step))) & ((row // step) != (col // step))
            first = [mm(jnp.where(take, low, 0.0), x) for low, x in zip(lowers, halves)]
            found = [f - mm(x, y) for f, x, y in zip(found, halves, first)]
        else:
            half_row = lax.broadcasted_iota(jnp.int32, (size // 2, size), 0)
            half_col = lax.broadcasted_iota(jnp.int32, (size // 2, size), 1)
            take = (half_col // step) == 2 * (half_row // step)
            first = [
                mm(jnp.where(take, odd_rows(low, step), 0.0), x) for low, x in zip(lowers, halves)
            ]
            odds = [odd_rows(f, step) for f in found]
            odds = [o - mm(o, with_odd_rows(zero, y, step)) for o, y in zip(odds, first)]
            found = [with_odd_rows(f, o, step) for f, o in zip(found, odds)]
        step *= 2
    return [x.astype(bf16) for x in found]


def layer_kernel(
    n1, n2, key_heads, ratio, hb,
    q_ref, k_ref, v_ref, qtap, ktap, vtap, beta_ref, decay_ref, gain_ref,
    q_hbm, k_hbm, v_hbm, gate_hbm, weight_hbm, out_ref,
    rates, rim, gate, weight, emitted, probing, msg, got, pre_m, pre_s, pre_a, start, ready, back, starting, gated, scaled,
    rim_send, rim_recv, load_sem, send_sem, recv_sem, chain_send, chain_recv, back_send, back_recv,
):
    step = pl.program_id(0)
    steps = pl.num_programs(0)
    me = lax.axis_index("ctx")
    tp = lax.axis_index("tp")
    total_devices = n1 * n2
    plane = me // n1
    place = me % n1
    base = plane * n1
    first, last = plane == 0, plane == n2 - 1
    rows = q_ref.shape[0]
    q_cols, v_cols = q_hbm.shape[1], v_hbm.shape[1]
    heads = key_heads * ratio
    per_step = heads // hb

    def at(index):
        return (index, tp)

    rim_cols = ((q_hbm, 0, q_cols), (k_hbm, q_cols, q_cols), (v_hbm, 2 * q_cols, v_cols))
    rim_copies = [
        pltpu.make_async_remote_copy(
            src_ref=source.at[pl.ds(rows - RIM, RIM)],
            dst_ref=rim.at[:, pl.ds(offset, width)],
            send_sem=rim_send.at[i],
            recv_sem=rim_recv.at[i],
            device_id=at((me + 1) % total_devices),
            device_id_type=MESH,
        )
        for i, (source, offset, width) in enumerate(rim_cols)
    ]
    weight_copy = pltpu.make_async_copy(weight_hbm, weight, load_sem.at[0])
    gate_copy = pltpu.make_async_copy(gate_hbm, gate, load_sem.at[1])

    @pl.when(step == 0)
    def _():
        barrier = pltpu.get_barrier_semaphore()

        def greet(index):
            pl.semaphore_signal(barrier, inc=1, device_id=at(index), device_id_type=MESH)

        partners = n1 - 1 + jnp.where(first, 0, 1) + jnp.where(last, 0, 1)
        for d in range(1, n1):
            greet(base + (place + d) % n1)

        @pl.when(jnp.logical_not(first))
        def _():
            greet(me - n1)

        @pl.when(jnp.logical_not(last))
        def _():
            greet(me + n1)

        if n1 > 1:
            before = jnp.logical_and(place == 0, me > 0)
            after = jnp.logical_and(place == n1 - 1, me < total_devices - 1)
            partners = partners + jnp.where(before, 1, 0) + jnp.where(after, 1, 0)

            @pl.when(before)
            def _():
                greet(me - 1)

            @pl.when(after)
            def _():
                greet(me + 1)

        pl.semaphore_wait(barrier, partners)

        @pl.when(me < total_devices - 1)
        def _():
            for copy in rim_copies:
                copy.start()

        gate_copy.start()
        weight_copy.start()
        sums = running_sums(decay_ref[...])
        for g in range(rates.shape[0]):
            rates[g, 0:heads] = sums[g * heads : (g + 1) * heads]
            rates[g, heads : 2 * heads] = beta_ref[g * heads : (g + 1) * heads, :]

        @pl.when(me == 0)
        def _():
            rim[...] = jnp.zeros_like(rim)

        @pl.when(me > 0)
        def _():
            for copy in rim_copies:
                copy.wait_recv()

    local_rates = rates[step]
    rate_cols = local_rates.T
    key_width, value_width = key_heads * DK, heads * DV

    def rim_part(offset, width):
        return rim[:, pl.ds(pl.multiple_of(offset + step * width, DK), width)].astype(f32)

    q_rim = rim_part(0, key_width)
    k_rim = rim_part(q_cols, key_width)
    v_rim = rim_part(2 * q_cols, value_width)
    row = lax.broadcasted_iota(jnp.int32, (rows, rows), 0)
    col = lax.broadcasted_iota(jnp.int32, (rows, rows), 1)
    sub = min(SUB, rows)
    count = rows // sub
    lowers, sims, rights, probes, tails, totals = [], [], [], [], [], []
    for g in range(key_heads):
        lo, hi = g * DK, (g + 1) * DK
        q = conv(q_ref, q_rim, qtap, lo, hi)
        k = conv(k_ref, k_rim, ktap, lo, hi)
        k = k * lax.rsqrt(jnp.sum(k * k, axis=-1, keepdims=True) + 1e-06)
        k_turned = k.T
        k_right = k_turned.astype(bf16)
        kk = mm(k, k_right)
        qk = mm(q, k_right)
        for r in range(ratio):
            h = g * ratio + r
            v = conv(v_ref, v_rim, vtap, h * DV, (h + 1) * DV)
            cum = rate_cols[:, h : h + 1]
            beta = rate_cols[:, heads + h : heads + h + 1]
            cum_row = local_rates[h : h + 1]
            fade = jnp.exp(jnp.minimum(cum - cum_row, 0.0))
            lowers.append(jnp.where(row > col, beta * fade * kk, 0.0))
            sims.append(jnp.where(row >= col, fade * qk, 0.0).astype(bf16))
            grown = jnp.exp(cum)
            rights.append(jnp.concatenate([beta * v, (beta * grown) * k], axis=1))
            probes.append(grown * q)
            end = cum_row[:, rows - 1 : rows]
            tails.append((k_turned * jnp.exp(end - cum_row)).astype(bf16))
            totals.append(jnp.exp(end))
    pieces = [
        low[i * sub : (i + 1) * sub, i * sub : (i + 1) * sub] for low in lowers for i in range(count)
    ]
    inverses = unit_lower_inverses(pieces)
    upper = lax.broadcasted_iota(jnp.int32, (EXTRA, DV), 0) < EXTRA // 2
    for h in range(heads):
        low = lowers[h]
        solved = []
        for i in range(count):
            right = rights[h][i * sub : (i + 1) * sub]
            if i > 0:
                before = jnp.concatenate(solved, axis=0)
                right = right - mm(low[i * sub : (i + 1) * sub, : i * sub], before)
            solved.append(mm(inverses[h * count + i], right).astype(bf16))
        solved = jnp.concatenate(solved, axis=0)
        seen = mm(sims[h], solved)
        lanes = pl.ds(pl.multiple_of((step * heads + h) * DV, DV), DV)
        emitted[:, lanes] = seen[:, :DV]
        probing[:, lanes] = (probes[h] - seen[:, DV:]).astype(bf16)
        update = mm(tails[h], solved)
        at_head = step * heads + h
        msg[at_head, 0:DK, :] = update[:, DV:].astype(bf16)
        msg[at_head, DK : 2 * DK, :] = update[:, :DV].astype(bf16)
        high, rest = split(jnp.broadcast_to(totals[h], (EXTRA, DV)))
        msg[at_head, 2 * DK :, :] = jnp.where(upper, high.astype(f32), rest.astype(f32)).astype(bf16)

    def map_copy(peer):
        return pltpu.make_async_remote_copy(
            src_ref=msg.at[pl.ds(peer * hb, hb)],
            dst_ref=got.at[place],
            send_sem=send_sem.at[peer],
            recv_sem=recv_sem.at[place],
            device_id=at(base + peer),
            device_id_type=MESH,
        )

    for j in range(per_step):
        peer = step * per_step + j

        @pl.when(peer != place)
        def _():
            map_copy(peer).start()

        @pl.when(peer == place)
        def _():
            pltpu.make_async_copy(
                msg.at[pl.ds(peer * hb, hb)], got.at[place], recv_sem.at[place]
            ).start()

    @pl.when(step == steps - 1)
    def _():
        maps = [jnp.zeros((DK, DK), f32) for _ in range(hb)]
        states = [jnp.zeros((DK, DV), f32) for _ in range(hb)]
        fades = [jnp.ones((1, DV), f32) for _ in range(hb)]
        eye_row = lax.broadcasted_iota(jnp.int32, (DK, DK), 0)
        eye_col = lax.broadcasted_iota(jnp.int32, (DK, DK), 1)
        eye = (eye_row == eye_col).astype(f32)
        for i in range(n1):
            pltpu.make_async_copy(got.at[i], got.at[i], recv_sem.at[i]).wait()
            for h in range(hb):
                pre_m[i, h] = maps[h].astype(bf16)
                pre_s[i, h] = states[h]
                pre_a[i, h] = jnp.broadcast_to(fades[h], (8, DV))
                m = got[i, h, 0:DK, :]
                s = got[i, h, DK : 2 * DK, :].astype(f32)
                tail = got[i, h, 2 * DK : 2 * DK + EXTRA, :].astype(f32)
                a = tail[0:1] + tail[EXTRA // 2 : EXTRA // 2 + 1]
                both = mm(m, jnp.concatenate([fades[h] * eye - maps[h], states[h]], axis=1))
                maps[h] = a * maps[h] + both[:, :DK]
                states[h] = a * states[h] - both[:, DK:] + s
                fades[h] = a * fades[h]

        @pl.when(first)
        def _():
            for h in range(hb):
                start[h] = jnp.zeros((DK, DV), bf16)

        def chain_copy(h):
            return pltpu.make_async_remote_copy(
                src_ref=ready.at[h],
                dst_ref=start.at[h],
                send_sem=chain_send.at[h],
                recv_sem=chain_recv.at[h],
                device_id=at((me + n1) % total_devices),
                device_id_type=MESH,
            )

        gain = gain_ref[...]

        def gate_part(h, carry):
            lanes = pl.ds(pl.multiple_of(h * DV, DV), DV)
            scaled[:, lanes] = gain * silu(gate[:, lanes].astype(f32))
            return carry

        gate_copy.wait()
        waits = 2 * plane >= n2

        @pl.when(waits)
        def _():
            lax.fori_loop(0, n1 * hb, gate_part, 0)

        for h in range(hb):
            @pl.when(jnp.logical_not(first))
            def _():
                chain_copy(h).wait_recv()

            @pl.when(jnp.logical_not(last))
            def _():
                begin = start[h]
                ready[h] = (
                    fades[h] * begin.astype(f32) - mm(maps[h], begin) + states[h]
                ).astype(bf16)
                chain_copy(h).start()

        for i in range(n1):
            for h in range(hb):
                begin = start[h]
                back[i, h] = (
                    pre_a[i, h, 0:1] * begin.astype(f32) - mm(pre_m[i, h], begin) + pre_s[i, h]
                ).astype(bf16)

        mine = pl.ds(place * hb, hb)
        returned = []
        for d in range(1, n1):
            peer = (place + d) % n1
            copy = pltpu.make_async_remote_copy(
                src_ref=back.at[peer],
                dst_ref=starting.at[mine],
                send_sem=back_send.at[d],
                recv_sem=back_recv.at[place],
                device_id=at(base + peer),
                device_id_type=MESH,
            )
            copy.start()
            returned.append(copy)
        pltpu.make_async_copy(back.at[place], starting.at[mine], back_recv.at[place]).start()

        @pl.when(jnp.logical_not(waits))
        def _():
            lax.fori_loop(0, n1 * hb, gate_part, 0)

        for i in range(n1):
            part = starting.at[pl.ds(i * hb, hb)]
            pltpu.make_async_copy(part, part, back_recv.at[i]).wait()
            for h in range(i * hb, (i + 1) * hb):
                lo, hi = h * DV, (h + 1) * DV
                core = emitted[:, lo:hi] + mm(probing[:, lo:hi], starting[h])
                scale = lax.rsqrt(jnp.mean(core * core, axis=-1, keepdims=True) + 1e-06)
                gated[:, lo:hi] = (core * scale * scaled[:, lo:hi]).astype(bf16)
        weight_copy.wait()
        width = out_ref.shape[1]
        tile = math.gcd(width, 512)

        def project(t, carry):
            lanes = pl.ds(pl.multiple_of(t * tile, tile), tile)
            out_ref[:, lanes] = jnp.dot(
                gated[...], weight[:, lanes], preferred_element_type=f32
            ).astype(bf16)
            return carry

        lax.fori_loop(0, width // tile, project, 0)
        for copy in returned:
            copy.wait_send()
        for peer in range(n1):
            @pl.when(peer != place)
            def _():
                map_copy(peer).wait_send()

        @pl.when(jnp.logical_not(last))
        def _():
            for h in range(hb):
                chain_copy(h).wait_send()

        @pl.when(me < total_devices - 1)
        def _():
            for copy in rim_copies:
                copy.wait_send()


def layer(n_ctx, query, key, value, gate, taps, beta, decay, gain, weight):
    rows, q_cols = query.shape
    v_cols = value.shape[1]
    key_heads, value_heads = q_cols // DK, v_cols // DV
    ratio = value_heads // key_heads
    n1 = math.gcd(math.gcd(value_heads, n_ctx), 8)
    n2 = n_ctx // n1
    hb = value_heads // n1
    step = math.gcd(key_heads, 2)
    while (step * ratio) % hb:
        step *= 2
    groups = key_heads // step
    heads = step * ratio
    kw, vw = step * DK, heads * DV
    width = weight.shape[1]
    wide = lambda n, size: pl.BlockSpec((n, size), lambda g: (0, g))
    whole = lambda shape: pl.BlockSpec(shape, lambda g: (0, 0))
    anywhere = pl.BlockSpec(memory_space=pl.ANY)
    count = taps[0].shape[0]
    return pl.pallas_call(
        functools.partial(layer_kernel, n1, n2, step, ratio, hb),
        grid=(groups,),
        in_specs=[
            wide(rows, kw), wide(rows, kw), wide(rows, vw),
            wide(count, kw), wide(count, kw), wide(count, vw),
            whole(beta.shape), whole(decay.shape), whole((1, DV)),
            anywhere, anywhere, anywhere, anywhere, anywhere,
        ],
        out_specs=whole((rows, width)),
        out_shape=jax.ShapeDtypeStruct((rows, width), bf16),
        scratch_shapes=[
            pltpu.VMEM((groups, 2 * heads, rows), f32),
            pltpu.VMEM((RIM, 2 * q_cols + v_cols), bf16),
            pltpu.VMEM(gate.shape, bf16),
            pltpu.VMEM(weight.shape, bf16),
            pltpu.VMEM((rows, v_cols), f32),
            pltpu.VMEM((rows, v_cols), bf16),
            pltpu.VMEM((value_heads, 2 * DK + EXTRA, DV), bf16),
            pltpu.VMEM((n1, hb, 2 * DK + EXTRA, DV), bf16),
            pltpu.VMEM((n1, hb, DK, DK), bf16),
            pltpu.VMEM((n1, hb, DK, DV), f32),
            pltpu.VMEM((n1, hb, 8, DV), f32),
            pltpu.VMEM((hb, DK, DV), bf16),
            pltpu.VMEM((hb, DK, DV), bf16),
            pltpu.VMEM((n1, hb, DK, DV), bf16),
            pltpu.VMEM((value_heads, DK, DV), bf16),
            pltpu.VMEM((rows, v_cols), bf16),
            pltpu.VMEM((rows, v_cols), f32),
            pltpu.SemaphoreType.DMA((3,)),
            pltpu.SemaphoreType.DMA((3,)),
            pltpu.SemaphoreType.DMA((2,)),
            pltpu.SemaphoreType.DMA((n1,)),
            pltpu.SemaphoreType.DMA((n1,)),
            pltpu.SemaphoreType.DMA((hb,)),
            pltpu.SemaphoreType.DMA((hb,)),
            pltpu.SemaphoreType.DMA((n1,)),
            pltpu.SemaphoreType.DMA((n1,)),
        ],
        compiler_params=pltpu.CompilerParams(
            collective_id=0, has_side_effects=True, vmem_limit_bytes=60 << 20
        ),
        name="layer",
    )(
        query, key, value, *taps, beta, decay, gain.reshape(1, DV),
        query, key, value, gate, weight,
    )


def local(
    n_ctx, n_tp,
    query_in, key_in, value_in, gate_values, query_conv, key_conv, value_conv,
    beta_rate, log_decay, norm_gain, out_weight,
):
    partial = layer(
        n_ctx, query_in, key_in, value_in, gate_values, (query_conv, key_conv, value_conv),
        beta_rate, log_decay, norm_gain, out_weight,
    )
    if n_tp == 1:
        return partial
    return lax.psum_scatter(partial, "tp", scatter_dimension=0, tiled=True)


def solution(mesh):
    return jax.shard_map(
        functools.partial(local, mesh.shape["ctx"], mesh.shape["tp"]),
        mesh=mesh,
        in_specs=(
            P("ctx", "tp"), P("ctx", "tp"), P("ctx", "tp"), P("ctx", "tp"),
            P(None, "tp"), P(None, "tp"), P(None, "tp"),
            P("tp", "ctx"), P("tp", "ctx"), P(), P("tp", None),
        ),
        out_specs=P(("ctx", "tp"), None),
        check_vma=False,
    )
```

```python
import functools
import math

import jax
import jax.numpy as jnp
from jax import lax
from jax.experimental import pallas as pl
from jax.experimental.pallas import tpu as pltpu
from jax.sharding import PartitionSpec as P

HK = 16
HV = 32
DK = 128
DV = 128
SUB = 128
RIM = 16
EXTRA = 16
MESH = pl.DeviceIdType.MESH
f32 = jnp.float32
bf16 = jnp.bfloat16


def mm(a, b):
    return jnp.dot(a.astype(bf16), b.astype(bf16), preferred_element_type=f32)


def split(a):
    high = a.astype(bf16)
    return high, (a - high.astype(f32)).astype(bf16)


def silu(x):
    return x / (1.0 + jnp.exp(-x))


def conv(raw_ref, rim, taps_ref, lo, hi):
    rows = raw_ref.shape[0]
    joined = jnp.concatenate([rim[RIM // 2 :, lo:hi], raw_ref[:, lo:hi].astype(f32)], axis=0)
    taps = taps_ref[:, lo:hi].astype(f32)
    count = taps.shape[0]
    first = RIM // 2 - count + 1
    total = taps[0:1] * joined[first : first + rows]
    for j in range(1, count):
        total = total + taps[j : j + 1] * joined[first + j : first + j + rows]
    return silu(total)


def running_sums(decay):
    rows = decay.shape[1]
    row = lax.broadcasted_iota(jnp.int32, (rows, rows), 0)
    col = lax.broadcasted_iota(jnp.int32, (rows, rows), 1)
    ones = (row <= col).astype(f32).astype(bf16)
    high, rest = split(decay)
    middle, low = split(decay - high.astype(f32))
    return mm(high, ones) + (mm(middle, ones) + mm(low, ones))


def odd_rows(x, step):
    count = x.shape[0] // (2 * step)
    return jnp.concatenate(
        [x[(2 * j + 1) * step : (2 * j + 2) * step] for j in range(count)], axis=0
    )


def with_odd_rows(even, odd, step):
    parts = []
    for j in range(odd.shape[0] // step):
        parts.append(even[2 * j * step : (2 * j + 1) * step])
        parts.append(odd[j * step : (j + 1) * step])
    return jnp.concatenate(parts, axis=0)


def unit_lower_inverses(lowers):
    size = lowers[0].shape[0]
    row = lax.broadcasted_iota(jnp.int32, (size, size), 0)
    col = lax.broadcasted_iota(jnp.int32, (size, size), 1)
    eye = (row == col).astype(f32)
    zero = jnp.zeros((size, size), f32)
    pair = ((row // 2) == (col // 2)) & (row != col)
    found = [eye - jnp.where(pair, low, 0.0) for low in lowers]
    step = 2
    while step < size:
        halves = [x.astype(bf16) for x in found]
        if step < 8:
            take = ((row // (2 * step)) == (col // (2 * step))) & ((row // step) != (col // step))
            first = [mm(jnp.where(take, low, 0.0), x) for low, x in zip(lowers, halves)]
            found = [f - mm(x, y) for f, x, y in zip(found, halves, first)]
        elif 2 * step == size:
            first = [mm(low[step:, :step], x[:step, :step]) for low, x in zip(lowers, halves)]
            corners = [mm(x[step:, step:], y) for x, y in zip(halves, first)]
            found = [
                jnp.concatenate(
                    [f[:step], jnp.concatenate([-c, f[step:, step:]], axis=1)], axis=0
                )
                for f, c in zip(found, corners)
            ]
        else:
            half_row = lax.broadcasted_iota(jnp.int32, (size // 2, size), 0)
            half_col = lax.broadcasted_iota(jnp.int32, (size // 2, size), 1)
            take = (half_col // step) == 2 * (half_row // step)
            first = [
                mm(jnp.where(take, odd_rows(low, step), 0.0), x) for low, x in zip(lowers, halves)
            ]
            odds = [odd_rows(f, step) for f in found]
            odds = [o - mm(o, with_odd_rows(zero, y, step)) for o, y in zip(odds, first)]
            found = [with_odd_rows(f, o, step) for f, o in zip(found, odds)]
        step *= 2
    return [x.astype(bf16) for x in found]


def layer_kernel(
    n1, n2, key_heads, ratio, hb,
    q_ref, k_ref, v_ref, qtap, ktap, vtap, beta_ref, decay_ref, gain_ref,
    q_hbm, k_hbm, v_hbm, gate_hbm, weight_hbm, out_ref,
    rates, rim, gate, weight, emitted, probing, msg, got, pre_m, pre_s, pre_a, start, ready, back, starting, gated, scaled,
    rim_send, rim_recv, load_sem, send_sem, recv_sem, chain_send, chain_recv, back_send, back_recv,
):
    step = pl.program_id(0)
    steps = pl.num_programs(0)
    me = lax.axis_index("ctx")
    tp = lax.axis_index("tp")
    total_devices = n1 * n2
    plane = me // n1
    place = me % n1
    base = plane * n1
    first, last = plane == 0, plane == n2 - 1
    rows = q_ref.shape[0]
    q_cols, v_cols = q_hbm.shape[1], v_hbm.shape[1]
    heads = key_heads * ratio
    per_step = heads // hb

    def at(index):
        return (index, tp)

    rim_cols = ((q_hbm, 0, q_cols), (k_hbm, q_cols, q_cols), (v_hbm, 2 * q_cols, v_cols))
    rim_copies = [
        pltpu.make_async_remote_copy(
            src_ref=source.at[pl.ds(rows - RIM, RIM)],
            dst_ref=rim.at[:, pl.ds(offset, width)],
            send_sem=rim_send.at[i],
            recv_sem=rim_recv.at[i],
            device_id=at((me + 1) % total_devices),
            device_id_type=MESH,
        )
        for i, (source, offset, width) in enumerate(rim_cols)
    ]
    weight_copy = pltpu.make_async_copy(weight_hbm, weight, load_sem.at[0])
    gate_copy = pltpu.make_async_copy(gate_hbm, gate, load_sem.at[1])

    @pl.when(step == 0)
    def _():
        barrier = pltpu.get_barrier_semaphore()

        def greet(index):
            pl.semaphore_signal(barrier, inc=1, device_id=at(index), device_id_type=MESH)

        partners = n1 - 1 + jnp.where(first, 0, 1) + jnp.where(last, 0, 1)
        for d in range(1, n1):
            greet(base + (place + d) % n1)

        @pl.when(jnp.logical_not(first))
        def _():
            greet(me - n1)

        @pl.when(jnp.logical_not(last))
        def _():
            greet(me + n1)

        if n1 > 1:
            before = jnp.logical_and(place == 0, me > 0)
            after = jnp.logical_and(place == n1 - 1, me < total_devices - 1)
            partners = partners + jnp.where(before, 1, 0) + jnp.where(after, 1, 0)

            @pl.when(before)
            def _():
                greet(me - 1)

            @pl.when(after)
            def _():
                greet(me + 1)

        pl.semaphore_wait(barrier, partners)

        @pl.when(me < total_devices - 1)
        def _():
            for copy in rim_copies:
                copy.start()

        gate_copy.start()
        weight_copy.start()
        sums = running_sums(decay_ref[...])
        for g in range(rates.shape[0]):
            rates[g, 0:heads] = sums[g * heads : (g + 1) * heads]
            rates[g, heads : 2 * heads] = beta_ref[g * heads : (g + 1) * heads, :]

        @pl.when(me == 0)
        def _():
            rim[...] = jnp.zeros_like(rim)

        @pl.when(me > 0)
        def _():
            for copy in rim_copies:
                copy.wait_recv()

    local_rates = rates[step]
    rate_cols = local_rates.T
    key_width, value_width = key_heads * DK, heads * DV

    def rim_part(offset, width):
        return rim[:, pl.ds(pl.multiple_of(offset + step * width, DK), width)].astype(f32)

    q_rim = rim_part(0, key_width)
    k_rim = rim_part(q_cols, key_width)
    v_rim = rim_part(2 * q_cols, value_width)
    row = lax.broadcasted_iota(jnp.int32, (rows, rows), 0)
    col = lax.broadcasted_iota(jnp.int32, (rows, rows), 1)
    sub = min(SUB, rows)
    count = rows // sub
    lowers, sims, rights, probes, tails, totals = [], [], [], [], [], []
    for g in range(key_heads):
        lo, hi = g * DK, (g + 1) * DK
        q = conv(q_ref, q_rim, qtap, lo, hi)
        k = conv(k_ref, k_rim, ktap, lo, hi)
        k = k * lax.rsqrt(jnp.sum(k * k, axis=-1, keepdims=True) + 1e-06)
        k_turned = k.T
        k_right = k_turned.astype(bf16)
        kk = mm(k, k_right)
        qk = mm(q, k_right)
        for r in range(ratio):
            h = g * ratio + r
            v = conv(v_ref, v_rim, vtap, h * DV, (h + 1) * DV)
            cum = rate_cols[:, h : h + 1]
            beta = rate_cols[:, heads + h : heads + h + 1]
            cum_row = local_rates[h : h + 1]
            fade = jnp.exp(jnp.minimum(cum - cum_row, 0.0))
            lowers.append(jnp.where(row > col, beta * fade * kk, 0.0))
            sims.append(jnp.where(row >= col, fade * qk, 0.0).astype(bf16))
            grown = jnp.exp(cum)
            rights.append(jnp.concatenate([beta * v, (beta * grown) * k], axis=1))
            probes.append(grown * q)
            end = cum_row[:, rows - 1 : rows]
            tails.append((k_turned * jnp.exp(end - cum_row)).astype(bf16))
            totals.append(jnp.exp(end))
    pieces = [
        low[i * sub : (i + 1) * sub, i * sub : (i + 1) * sub] for low in lowers for i in range(count)
    ]
    inverses = unit_lower_inverses(pieces)
    upper = lax.broadcasted_iota(jnp.int32, (EXTRA, DV), 0) < EXTRA // 2
    for h in range(heads):
        low = lowers[h]
        solved = []
        for i in range(count):
            right = rights[h][i * sub : (i + 1) * sub]
            if i > 0:
                before = jnp.concatenate(solved, axis=0)
                right = right - mm(low[i * sub : (i + 1) * sub, : i * sub], before)
            solved.append(mm(inverses[h * count + i], right).astype(bf16))
        solved = jnp.concatenate(solved, axis=0)
        seen = mm(sims[h], solved)
        lanes = pl.ds(pl.multiple_of((step * heads + h) * DV, DV), DV)
        emitted[:, lanes] = seen[:, :DV]
        probing[:, lanes] = (probes[h] - seen[:, DV:]).astype(bf16)
        update = mm(tails[h], solved)
        at_head = step * heads + h
        msg[at_head, 0:DK, :] = update[:, DV:].astype(bf16)
        msg[at_head, DK : 2 * DK, :] = update[:, :DV].astype(bf16)
        high, rest = split(jnp.broadcast_to(totals[h], (EXTRA, DV)))
        msg[at_head, 2 * DK :, :] = jnp.where(upper, high.astype(f32), rest.astype(f32)).astype(bf16)

    def map_copy(peer):
        return pltpu.make_async_remote_copy(
            src_ref=msg.at[pl.ds(peer * hb, hb)],
            dst_ref=got.at[place],
            send_sem=send_sem.at[peer],
            recv_sem=recv_sem.at[place],
            device_id=at(base + peer),
            device_id_type=MESH,
        )

    for j in range(per_step):
        peer = step * per_step + j

        @pl.when(peer != place)
        def _():
            map_copy(peer).start()

        @pl.when(peer == place)
        def _():
            pltpu.make_async_copy(
                msg.at[pl.ds(peer * hb, hb)], got.at[place], recv_sem.at[place]
            ).start()

    @pl.when(step == steps - 1)
    def _():
        maps = [jnp.zeros((DK, DK), f32) for _ in range(hb)]
        states = [jnp.zeros((DK, DV), f32) for _ in range(hb)]
        fades = [jnp.ones((1, DV), f32) for _ in range(hb)]
        eye_row = lax.broadcasted_iota(jnp.int32, (DK, DK), 0)
        eye_col = lax.broadcasted_iota(jnp.int32, (DK, DK), 1)
        eye = (eye_row == eye_col).astype(f32)
        for i in range(n1):
            pltpu.make_async_copy(got.at[i], got.at[i], recv_sem.at[i]).wait()
            for h in range(hb):
                pre_m[i, h] = maps[h].astype(bf16)
                pre_s[i, h] = states[h]
                pre_a[i, h] = jnp.broadcast_to(fades[h], (8, DV))
                m = got[i, h, 0:DK, :]
                s = got[i, h, DK : 2 * DK, :].astype(f32)
                tail = got[i, h, 2 * DK : 2 * DK + EXTRA, :].astype(f32)
                a = tail[0:1] + tail[EXTRA // 2 : EXTRA // 2 + 1]
                both = mm(m, jnp.concatenate([fades[h] * eye - maps[h], states[h]], axis=1))
                maps[h] = a * maps[h] + both[:, :DK]
                states[h] = a * states[h] - both[:, DK:] + s
                fades[h] = a * fades[h]

        @pl.when(first)
        def _():
            for h in range(hb):
                start[h] = jnp.zeros((DK, DV), bf16)

        def chain_copy(h):
            return pltpu.make_async_remote_copy(
                src_ref=ready.at[h],
                dst_ref=start.at[h],
                send_sem=chain_send.at[h],
                recv_sem=chain_recv.at[h],
                device_id=at((me + n1) % total_devices),
                device_id_type=MESH,
            )

        gain = gain_ref[...]

        def gate_part(h, carry):
            lanes = pl.ds(pl.multiple_of(h * DV, DV), DV)
            scaled[:, lanes] = gain * silu(gate[:, lanes].astype(f32))
            return carry

        gate_copy.wait()
        waits = 2 * plane >= n2

        @pl.when(waits)
        def _():
            lax.fori_loop(0, n1 * hb, gate_part, 0)

        for h in range(hb):
            @pl.when(jnp.logical_not(first))
            def _():
                chain_copy(h).wait_recv()

            @pl.when(jnp.logical_not(last))
            def _():
                begin = start[h]
                ready[h] = (
                    fades[h] * begin.astype(f32) - mm(maps[h], begin) + states[h]
                ).astype(bf16)
                chain_copy(h).start()

        for i in range(n1):
            for h in range(hb):
                begin = start[h]
                back[i, h] = (
                    pre_a[i, h, 0:1] * begin.astype(f32) - mm(pre_m[i, h], begin) + pre_s[i, h]
                ).astype(bf16)

        mine = pl.ds(place * hb, hb)
        returned = []
        for d in range(1, n1):
            peer = (place + d) % n1
            copy = pltpu.make_async_remote_copy(
                src_ref=back.at[peer],
                dst_ref=starting.at[mine],
                send_sem=back_send.at[d],
                recv_sem=back_recv.at[place],
                device_id=at(base + peer),
                device_id_type=MESH,
            )
            copy.start()
            returned.append(copy)
        pltpu.make_async_copy(back.at[place], starting.at[mine], back_recv.at[place]).start()

        @pl.when(jnp.logical_not(waits))
        def _():
            lax.fori_loop(0, n1 * hb, gate_part, 0)

        for i in range(n1):
            part = starting.at[pl.ds(i * hb, hb)]
            pltpu.make_async_copy(part, part, back_recv.at[i]).wait()
            for h in range(i * hb, (i + 1) * hb):
                lo, hi = h * DV, (h + 1) * DV
                core = emitted[:, lo:hi] + mm(probing[:, lo:hi], starting[h])
                scale = lax.rsqrt(jnp.mean(core * core, axis=-1, keepdims=True) + 1e-06)
                gated[:, lo:hi] = (core * scale * scaled[:, lo:hi]).astype(bf16)
        weight_copy.wait()
        width = out_ref.shape[1]
        tile = math.gcd(width, 512)

        def project(t, carry):
            lanes = pl.ds(pl.multiple_of(t * tile, tile), tile)
            out_ref[:, lanes] = jnp.dot(
                gated[...], weight[:, lanes], preferred_element_type=f32
            ).astype(bf16)
            return carry

        lax.fori_loop(0, width // tile, project, 0)
        for copy in returned:
            copy.wait_send()
        for peer in range(n1):
            @pl.when(peer != place)
            def _():
                map_copy(peer).wait_send()

        @pl.when(jnp.logical_not(last))
        def _():
            for h in range(hb):
                chain_copy(h).wait_send()

        @pl.when(me < total_devices - 1)
        def _():
            for copy in rim_copies:
                copy.wait_send()


def layer(n_ctx, query, key, value, gate, taps, beta, decay, gain, weight):
    rows, q_cols = query.shape
    v_cols = value.shape[1]
    key_heads, value_heads = q_cols // DK, v_cols // DV
    ratio = value_heads // key_heads
    n1 = math.gcd(math.gcd(value_heads, n_ctx), 8)
    n2 = n_ctx // n1
    hb = value_heads // n1
    step = math.gcd(key_heads, 4)
    while (step * ratio) % hb:
        step *= 2
    groups = key_heads // step
    heads = step * ratio
    kw, vw = step * DK, heads * DV
    width = weight.shape[1]
    wide = lambda n, size: pl.BlockSpec((n, size), lambda g: (0, g))
    whole = lambda shape: pl.BlockSpec(shape, lambda g: (0, 0))
    anywhere = pl.BlockSpec(memory_space=pl.ANY)
    count = taps[0].shape[0]
    return pl.pallas_call(
        functools.partial(layer_kernel, n1, n2, step, ratio, hb),
        grid=(groups,),
        in_specs=[
            wide(rows, kw), wide(rows, kw), wide(rows, vw),
            wide(count, kw), wide(count, kw), wide(count, vw),
            whole(beta.shape), whole(decay.shape), whole((1, DV)),
            anywhere, anywhere, anywhere, anywhere, anywhere,
        ],
        out_specs=whole((rows, width)),
        out_shape=jax.ShapeDtypeStruct((rows, width), bf16),
        scratch_shapes=[
            pltpu.VMEM((groups, 2 * heads, rows), f32),
            pltpu.VMEM((RIM, 2 * q_cols + v_cols), bf16),
            pltpu.VMEM(gate.shape, bf16),
            pltpu.VMEM(weight.shape, bf16),
            pltpu.VMEM((rows, v_cols), f32),
            pltpu.VMEM((rows, v_cols), bf16),
            pltpu.VMEM((value_heads, 2 * DK + EXTRA, DV), bf16),
            pltpu.VMEM((n1, hb, 2 * DK + EXTRA, DV), bf16),
            pltpu.VMEM((n1, hb, DK, DK), bf16),
            pltpu.VMEM((n1, hb, DK, DV), f32),
            pltpu.VMEM((n1, hb, 8, DV), f32),
            pltpu.VMEM((hb, DK, DV), bf16),
            pltpu.VMEM((hb, DK, DV), bf16),
            pltpu.VMEM((n1, hb, DK, DV), bf16),
            pltpu.VMEM((value_heads, DK, DV), bf16),
            pltpu.VMEM((rows, v_cols), bf16),
            pltpu.VMEM((rows, v_cols), f32),
            pltpu.SemaphoreType.DMA((3,)),
            pltpu.SemaphoreType.DMA((3,)),
            pltpu.SemaphoreType.DMA((2,)),
            pltpu.SemaphoreType.DMA((n1,)),
            pltpu.SemaphoreType.DMA((n1,)),
            pltpu.SemaphoreType.DMA((hb,)),
            pltpu.SemaphoreType.DMA((hb,)),
            pltpu.SemaphoreType.DMA((n1,)),
            pltpu.SemaphoreType.DMA((n1,)),
        ],
        compiler_params=pltpu.CompilerParams(
            collective_id=0, has_side_effects=True, vmem_limit_bytes=60 << 20
        ),
        name="layer",
    )(
        query, key, value, *taps, beta, decay, gain.reshape(1, DV),
        query, key, value, gate, weight,
    )


def local(
    n_ctx, n_tp,
    query_in, key_in, value_in, gate_values, query_conv, key_conv, value_conv,
    beta_rate, log_decay, norm_gain, out_weight,
):
    partial = layer(
        n_ctx, query_in, key_in, value_in, gate_values, (query_conv, key_conv, value_conv),
        beta_rate, log_decay, norm_gain, out_weight,
    )
    if n_tp == 1:
        return partial
    return lax.psum_scatter(partial, "tp", scatter_dimension=0, tiled=True)


def solution(mesh):
    return jax.shard_map(
        functools.partial(local, mesh.shape["ctx"], mesh.shape["tp"]),
        mesh=mesh,
        in_specs=(
            P("ctx", "tp"), P("ctx", "tp"), P("ctx", "tp"), P("ctx", "tp"),
            P(None, "tp"), P(None, "tp"), P(None, "tp"),
            P("tp", "ctx"), P("tp", "ctx"), P(), P("tp", None),
        ),
        out_specs=P(("ctx", "tp"), None),
        check_vma=False,
    )
```

```python
import functools
import math

import jax
import jax.numpy as jnp
from jax import lax
from jax.experimental import pallas as pl
from jax.experimental.pallas import tpu as pltpu
from jax.sharding import PartitionSpec as P

HK = 16
HV = 32
DK = 128
DV = 128
SUB = 128
RIM = 16
EXTRA = 16
MESH = pl.DeviceIdType.MESH
f32 = jnp.float32
bf16 = jnp.bfloat16


def mm(a, b):
    return jnp.dot(a.astype(bf16), b.astype(bf16), preferred_element_type=f32)


def split(a):
    high = a.astype(bf16)
    return high, (a - high.astype(f32)).astype(bf16)


def silu(x):
    half = 0.5 * x
    return half + half * jnp.tanh(half)


def conv(raw_ref, rim, taps_ref, lo, hi):
    rows = raw_ref.shape[0]
    joined = jnp.concatenate([rim[RIM // 2 :, lo:hi], raw_ref[:, lo:hi].astype(f32)], axis=0)
    taps = taps_ref[:, lo:hi].astype(f32)
    count = taps.shape[0]
    first = RIM // 2 - count + 1
    total = taps[0:1] * joined[first : first + rows]
    for j in range(1, count):
        total = total + taps[j : j + 1] * joined[first + j : first + j + rows]
    return silu(total)


def running_sums(decay):
    rows = decay.shape[1]
    row = lax.broadcasted_iota(jnp.int32, (rows, rows), 0)
    col = lax.broadcasted_iota(jnp.int32, (rows, rows), 1)
    ones = (row <= col).astype(f32).astype(bf16)
    high, rest = split(decay)
    middle, low = split(decay - high.astype(f32))
    return mm(high, ones) + (mm(middle, ones) + mm(low, ones))


def odd_rows(x, step):
    count = x.shape[0] // (2 * step)
    return jnp.concatenate(
        [x[(2 * j + 1) * step : (2 * j + 2) * step] for j in range(count)], axis=0
    )


def with_odd_rows(even, odd, step):
    parts = []
    for j in range(odd.shape[0] // step):
        parts.append(even[2 * j * step : (2 * j + 1) * step])
        parts.append(odd[j * step : (j + 1) * step])
    return jnp.concatenate(parts, axis=0)


def unit_lower_inverses(lowers):
    size = lowers[0].shape[0]
    row = lax.broadcasted_iota(jnp.int32, (size, size), 0)
    col = lax.broadcasted_iota(jnp.int32, (size, size), 1)
    eye = (row == col).astype(f32)
    zero = jnp.zeros((size, size), f32)
    pair = ((row // 2) == (col // 2)) & (row != col)
    found = [eye - jnp.where(pair, low, 0.0) for low in lowers]
    step = 2
    while step < size:
        halves = [x.astype(bf16) for x in found]
        if step < 8:
            take = ((row // (2 * step)) == (col // (2 * step))) & ((row // step) != (col // step))
            first = [mm(jnp.where(take, low, 0.0), x) for low, x in zip(lowers, halves)]
            found = [f - mm(x, y) for f, x, y in zip(found, halves, first)]
        elif 2 * step == size:
            first = [mm(low[step:, :step], x[:step, :step]) for low, x in zip(lowers, halves)]
            corners = [mm(x[step:, step:], y) for x, y in zip(halves, first)]
            found = [
                jnp.concatenate(
                    [f[:step], jnp.concatenate([-c, f[step:, step:]], axis=1)], axis=0
                )
                for f, c in zip(found, corners)
            ]
        else:
            half_row = lax.broadcasted_iota(jnp.int32, (size // 2, size), 0)
            half_col = lax.broadcasted_iota(jnp.int32, (size // 2, size), 1)
            take = (half_col // step) == 2 * (half_row // step)
            first = [
                mm(jnp.where(take, odd_rows(low, step), 0.0), x) for low, x in zip(lowers, halves)
            ]
            odds = [odd_rows(f, step) for f in found]
            odds = [o - mm(o, with_odd_rows(zero, y, step)) for o, y in zip(odds, first)]
            found = [with_odd_rows(f, o, step) for f, o in zip(found, odds)]
        step *= 2
    return [x.astype(bf16) for x in found]


def layer_kernel(
    n1, n2, key_heads, ratio, hb,
    q_ref, k_ref, v_ref, qtap, ktap, vtap, beta_ref, decay_ref, gain_ref,
    q_hbm, k_hbm, v_hbm, gate_hbm, weight_hbm, out_ref,
    rates, rim, gate, weight, emitted, probing, msg, got, pre_m, pre_s, pre_a, start, ready, back, starting, gated, scaled,
    rim_send, rim_recv, load_sem, send_sem, recv_sem, chain_send, chain_recv, back_send, back_recv,
):
    step = pl.program_id(0)
    steps = pl.num_programs(0)
    me = lax.axis_index("ctx")
    tp = lax.axis_index("tp")
    total_devices = n1 * n2
    plane = me // n1
    place = me % n1
    base = plane * n1
    first, last = plane == 0, plane == n2 - 1
    rows = q_ref.shape[0]
    q_cols, v_cols = q_hbm.shape[1], v_hbm.shape[1]
    heads = key_heads * ratio
    per_step = heads // hb

    def at(index):
        return (index, tp)

    rim_cols = ((q_hbm, 0, q_cols), (k_hbm, q_cols, q_cols), (v_hbm, 2 * q_cols, v_cols))
    rim_copies = [
        pltpu.make_async_remote_copy(
            src_ref=source.at[pl.ds(rows - RIM, RIM)],
            dst_ref=rim.at[:, pl.ds(offset, width)],
            send_sem=rim_send.at[i],
            recv_sem=rim_recv.at[i],
            device_id=at((me + 1) % total_devices),
            device_id_type=MESH,
        )
        for i, (source, offset, width) in enumerate(rim_cols)
    ]
    weight_copy = pltpu.make_async_copy(weight_hbm, weight, load_sem.at[0])
    gate_copy = pltpu.make_async_copy(gate_hbm, gate, load_sem.at[1])

    @pl.when(step == 0)
    def _():
        barrier = pltpu.get_barrier_semaphore()

        def greet(index):
            pl.semaphore_signal(barrier, inc=1, device_id=at(index), device_id_type=MESH)

        partners = n1 - 1 + jnp.where(first, 0, 1) + jnp.where(last, 0, 1)
        for d in range(1, n1):
            greet(base + (place + d) % n1)

        @pl.when(jnp.logical_not(first))
        def _():
            greet(me - n1)

        @pl.when(jnp.logical_not(last))
        def _():
            greet(me + n1)

        if n1 > 1:
            before = jnp.logical_and(place == 0, me > 0)
            after = jnp.logical_and(place == n1 - 1, me < total_devices - 1)
            partners = partners + jnp.where(before, 1, 0) + jnp.where(after, 1, 0)

            @pl.when(before)
            def _():
                greet(me - 1)

            @pl.when(after)
            def _():
                greet(me + 1)

        pl.semaphore_wait(barrier, partners)

        @pl.when(me < total_devices - 1)
        def _():
            for copy in rim_copies:
                copy.start()

        gate_copy.start()
        weight_copy.start()
        sums = running_sums(decay_ref[...])
        for g in range(rates.shape[0]):
            rates[g, 0:heads] = sums[g * heads : (g + 1) * heads]
            rates[g, heads : 2 * heads] = beta_ref[g * heads : (g + 1) * heads, :]

        @pl.when(me == 0)
        def _():
            rim[...] = jnp.zeros_like(rim)

        @pl.when(me > 0)
        def _():
            for copy in rim_copies:
                copy.wait_recv()

    local_rates = rates[step]
    rate_cols = local_rates.T
    key_width, value_width = key_heads * DK, heads * DV

    def rim_part(offset, width):
        return rim[:, pl.ds(pl.multiple_of(offset + step * width, DK), width)].astype(f32)

    q_rim = rim_part(0, key_width)
    k_rim = rim_part(q_cols, key_width)
    v_rim = rim_part(2 * q_cols, value_width)
    row = lax.broadcasted_iota(jnp.int32, (rows, rows), 0)
    col = lax.broadcasted_iota(jnp.int32, (rows, rows), 1)
    sub = min(SUB, rows)
    count = rows // sub
    lowers, sims, rights, probes, tails, totals = [], [], [], [], [], []
    for g in range(key_heads):
        lo, hi = g * DK, (g + 1) * DK
        q = conv(q_ref, q_rim, qtap, lo, hi)
        k = conv(k_ref, k_rim, ktap, lo, hi)
        k = k * lax.rsqrt(jnp.sum(k * k, axis=-1, keepdims=True) + 1e-06)
        k_turned = k.T
        k_right = k_turned.astype(bf16)
        kk = mm(k, k_right)
        qk = mm(q, k_right)
        for r in range(ratio):
            h = g * ratio + r
            v = conv(v_ref, v_rim, vtap, h * DV, (h + 1) * DV)
            cum = rate_cols[:, h : h + 1]
            beta = rate_cols[:, heads + h : heads + h + 1]
            cum_row = local_rates[h : h + 1]
            fade = jnp.exp(jnp.minimum(cum - cum_row, 0.0))
            lowers.append(jnp.where(row > col, beta * fade * kk, 0.0))
            sims.append(jnp.where(row >= col, fade * qk, 0.0).astype(bf16))
            grown = jnp.exp(cum)
            rights.append(jnp.concatenate([beta * v, (beta * grown) * k], axis=1))
            probes.append(grown * q)
            end = cum_row[:, rows - 1 : rows]
            tails.append((k_turned * jnp.exp(end - cum_row)).astype(bf16))
            totals.append(jnp.exp(end))
    pieces = [
        low[i * sub : (i + 1) * sub, i * sub : (i + 1) * sub] for low in lowers for i in range(count)
    ]
    inverses = unit_lower_inverses(pieces)
    upper = lax.broadcasted_iota(jnp.int32, (EXTRA, DV), 0) < EXTRA // 2
    for h in range(heads):
        low = lowers[h]
        solved = []
        for i in range(count):
            right = rights[h][i * sub : (i + 1) * sub]
            if i > 0:
                before = jnp.concatenate(solved, axis=0)
                right = right - mm(low[i * sub : (i + 1) * sub, : i * sub], before)
            solved.append(mm(inverses[h * count + i], right).astype(bf16))
        solved = jnp.concatenate(solved, axis=0)
        seen = mm(sims[h], solved)
        lanes = pl.ds(pl.multiple_of((step * heads + h) * DV, DV), DV)
        emitted[:, lanes] = seen[:, :DV]
        probing[:, lanes] = (probes[h] - seen[:, DV:]).astype(bf16)
        update = mm(tails[h], solved)
        at_head = step * heads + h
        msg[at_head, 0:DK, :] = update[:, DV:].astype(bf16)
        msg[at_head, DK : 2 * DK, :] = update[:, :DV].astype(bf16)
        high, rest = split(jnp.broadcast_to(totals[h], (EXTRA, DV)))
        msg[at_head, 2 * DK :, :] = jnp.where(upper, high.astype(f32), rest.astype(f32)).astype(bf16)

    def map_copy(peer):
        return pltpu.make_async_remote_copy(
            src_ref=msg.at[pl.ds(peer * hb, hb)],
            dst_ref=got.at[place],
            send_sem=send_sem.at[peer],
            recv_sem=recv_sem.at[place],
            device_id=at(base + peer),
            device_id_type=MESH,
        )

    for j in range(per_step):
        peer = step * per_step + j

        @pl.when(peer != place)
        def _():
            map_copy(peer).start()

        @pl.when(peer == place)
        def _():
            pltpu.make_async_copy(
                msg.at[pl.ds(peer * hb, hb)], got.at[place], recv_sem.at[place]
            ).start()

    @pl.when(step == steps - 1)
    def _():
        maps = [jnp.zeros((DK, DK), f32) for _ in range(hb)]
        states = [jnp.zeros((DK, DV), f32) for _ in range(hb)]
        fades = [jnp.ones((1, DV), f32) for _ in range(hb)]
        eye_row = lax.broadcasted_iota(jnp.int32, (DK, DK), 0)
        eye_col = lax.broadcasted_iota(jnp.int32, (DK, DK), 1)
        eye = (eye_row == eye_col).astype(f32)
        for i in range(n1):
            pltpu.make_async_copy(got.at[i], got.at[i], recv_sem.at[i]).wait()
            for h in range(hb):
                pre_m[i, h] = maps[h].astype(bf16)
                pre_s[i, h] = states[h]
                pre_a[i, h] = jnp.broadcast_to(fades[h], (8, DV))
                m = got[i, h, 0:DK, :]
                s = got[i, h, DK : 2 * DK, :].astype(f32)
                tail = got[i, h, 2 * DK : 2 * DK + EXTRA, :].astype(f32)
                a = tail[0:1] + tail[EXTRA // 2 : EXTRA // 2 + 1]
                both = mm(m, jnp.concatenate([fades[h] * eye - maps[h], states[h]], axis=1))
                maps[h] = a * maps[h] + both[:, :DK]
                states[h] = a * states[h] - both[:, DK:] + s
                fades[h] = a * fades[h]

        @pl.when(first)
        def _():
            for h in range(hb):
                start[h] = jnp.zeros((DK, DV), bf16)

        def chain_copy(h):
            return pltpu.make_async_remote_copy(
                src_ref=ready.at[h],
                dst_ref=start.at[h],
                send_sem=chain_send.at[h],
                recv_sem=chain_recv.at[h],
                device_id=at((me + n1) % total_devices),
                device_id_type=MESH,
            )

        gain = gain_ref[...]

        def gate_part(h, carry):
            lanes = pl.ds(pl.multiple_of(h * DV, DV), DV)
            scaled[:, lanes] = gain * silu(gate[:, lanes].astype(f32))
            return carry

        gate_copy.wait()
        waits = 2 * plane >= n2

        @pl.when(waits)
        def _():
            lax.fori_loop(0, n1 * hb, gate_part, 0)

        for h in range(hb):
            @pl.when(jnp.logical_not(first))
            def _():
                chain_copy(h).wait_recv()

            @pl.when(jnp.logical_not(last))
            def _():
                begin = start[h]
                ready[h] = (
                    fades[h] * begin.astype(f32) - mm(maps[h], begin) + states[h]
                ).astype(bf16)
                chain_copy(h).start()

        for i in range(n1):
            for h in range(hb):
                begin = start[h]
                back[i, h] = (
                    pre_a[i, h, 0:1] * begin.astype(f32) - mm(pre_m[i, h], begin) + pre_s[i, h]
                ).astype(bf16)

        mine = pl.ds(place * hb, hb)
        returned = []
        for d in range(1, n1):
            peer = (place + d) % n1
            copy = pltpu.make_async_remote_copy(
                src_ref=back.at[peer],
                dst_ref=starting.at[mine],
                send_sem=back_send.at[d],
                recv_sem=back_recv.at[place],
                device_id=at(base + peer),
                device_id_type=MESH,
            )
            copy.start()
            returned.append(copy)
        pltpu.make_async_copy(back.at[place], starting.at[mine], back_recv.at[place]).start()

        @pl.when(jnp.logical_not(waits))
        def _():
            lax.fori_loop(0, n1 * hb, gate_part, 0)

        for i in range(n1):
            part = starting.at[pl.ds(i * hb, hb)]
            pltpu.make_async_copy(part, part, back_recv.at[i]).wait()
            for h in range(i * hb, (i + 1) * hb):
                lo, hi = h * DV, (h + 1) * DV
                core = emitted[:, lo:hi] + mm(probing[:, lo:hi], starting[h])
                scale = lax.rsqrt(jnp.mean(core * core, axis=-1, keepdims=True) + 1e-06)
                gated[:, lo:hi] = (core * scale * scaled[:, lo:hi]).astype(bf16)
        weight_copy.wait()
        width = out_ref.shape[1]
        tile = math.gcd(width, 512)

        def project(t, carry):
            lanes = pl.ds(pl.multiple_of(t * tile, tile), tile)
            out_ref[:, lanes] = jnp.dot(
                gated[...], weight[:, lanes], preferred_element_type=f32
            ).astype(bf16)
            return carry

        lax.fori_loop(0, width // tile, project, 0)
        for copy in returned:
            copy.wait_send()
        for peer in range(n1):
            @pl.when(peer != place)
            def _():
                map_copy(peer).wait_send()

        @pl.when(jnp.logical_not(last))
        def _():
            for h in range(hb):
                chain_copy(h).wait_send()

        @pl.when(me < total_devices - 1)
        def _():
            for copy in rim_copies:
                copy.wait_send()


def layer(n_ctx, query, key, value, gate, taps, beta, decay, gain, weight):
    rows, q_cols = query.shape
    v_cols = value.shape[1]
    key_heads, value_heads = q_cols // DK, v_cols // DV
    ratio = value_heads // key_heads
    n1 = math.gcd(math.gcd(value_heads, n_ctx), 8)
    n2 = n_ctx // n1
    hb = value_heads // n1
    step = math.gcd(key_heads, 4)
    while (step * ratio) % hb:
        step *= 2
    groups = key_heads // step
    heads = step * ratio
    kw, vw = step * DK, heads * DV
    width = weight.shape[1]
    wide = lambda n, size: pl.BlockSpec((n, size), lambda g: (0, g))
    whole = lambda shape: pl.BlockSpec(shape, lambda g: (0, 0))
    anywhere = pl.BlockSpec(memory_space=pl.ANY)
    count = taps[0].shape[0]
    return pl.pallas_call(
        functools.partial(layer_kernel, n1, n2, step, ratio, hb),
        grid=(groups,),
        in_specs=[
            wide(rows, kw), wide(rows, kw), wide(rows, vw),
            wide(count, kw), wide(count, kw), wide(count, vw),
            whole(beta.shape), whole(decay.shape), whole((1, DV)),
            anywhere, anywhere, anywhere, anywhere, anywhere,
        ],
        out_specs=whole((rows, width)),
        out_shape=jax.ShapeDtypeStruct((rows, width), bf16),
        scratch_shapes=[
            pltpu.VMEM((groups, 2 * heads, rows), f32),
            pltpu.VMEM((RIM, 2 * q_cols + v_cols), bf16),
            pltpu.VMEM(gate.shape, bf16),
            pltpu.VMEM(weight.shape, bf16),
            pltpu.VMEM((rows, v_cols), f32),
            pltpu.VMEM((rows, v_cols), bf16),
            pltpu.VMEM((value_heads, 2 * DK + EXTRA, DV), bf16),
            pltpu.VMEM((n1, hb, 2 * DK + EXTRA, DV), bf16),
            pltpu.VMEM((n1, hb, DK, DK), bf16),
            pltpu.VMEM((n1, hb, DK, DV), f32),
            pltpu.VMEM((n1, hb, 8, DV), f32),
            pltpu.VMEM((hb, DK, DV), bf16),
            pltpu.VMEM((hb, DK, DV), bf16),
            pltpu.VMEM((n1, hb, DK, DV), bf16),
            pltpu.VMEM((value_heads, DK, DV), bf16),
            pltpu.VMEM((rows, v_cols), bf16),
            pltpu.VMEM((rows, v_cols), f32),
            pltpu.SemaphoreType.DMA((3,)),
            pltpu.SemaphoreType.DMA((3,)),
            pltpu.SemaphoreType.DMA((2,)),
            pltpu.SemaphoreType.DMA((n1,)),
            pltpu.SemaphoreType.DMA((n1,)),
            pltpu.SemaphoreType.DMA((hb,)),
            pltpu.SemaphoreType.DMA((hb,)),
            pltpu.SemaphoreType.DMA((n1,)),
            pltpu.SemaphoreType.DMA((n1,)),
        ],
        compiler_params=pltpu.CompilerParams(
            collective_id=0, has_side_effects=True, vmem_limit_bytes=60 << 20
        ),
        name="layer",
    )(
        query, key, value, *taps, beta, decay, gain.reshape(1, DV),
        query, key, value, gate, weight,
    )


def local(
    n_ctx, n_tp,
    query_in, key_in, value_in, gate_values, query_conv, key_conv, value_conv,
    beta_rate, log_decay, norm_gain, out_weight,
):
    partial = layer(
        n_ctx, query_in, key_in, value_in, gate_values, (query_conv, key_conv, value_conv),
        beta_rate, log_decay, norm_gain, out_weight,
    )
    if n_tp == 1:
        return partial
    return lax.psum_scatter(partial, "tp", scatter_dimension=0, tiled=True)


def solution(mesh):
    return jax.shard_map(
        functools.partial(local, mesh.shape["ctx"], mesh.shape["tp"]),
        mesh=mesh,
        in_specs=(
            P("ctx", "tp"), P("ctx", "tp"), P("ctx", "tp"), P("ctx", "tp"),
            P(None, "tp"), P(None, "tp"), P(None, "tp"),
            P("tp", "ctx"), P("tp", "ctx"), P(), P("tp", None),
        ),
        out_specs=P(("ctx", "tp"), None),
        check_vma=False,
    )
```
